128 devices in a mesh: dp: 32 (over z, y, core), ctx: 4 (over x).
Axes of the slice: x: 4, y: 4, z: 4, core: 2. Of those that a mesh axis runs over, the one named last changes fastest.
Arguments:
- q_rows: bfloat16 [16384, 8192], P(('dp', 'ctx')), may hold values from -6 to 6
- k_rows: bfloat16 [16384, 8192], P(('dp', 'ctx')), may hold values from -6 to 6
- v_rows: bfloat16 [16384, 8192], P(('dp', 'ctx')), may hold values from -6 to 6
- out_grad: bfloat16 [16384, 8192], P(('dp', 'ctx')), may hold values from -24 to 24
- filters: float32 [512, 128], replicated, may hold values from -0.5 to 0.5
- skip_gain: float32 [8192], replicated, may hold values from -4 to 4
- genome_len: int32 [32, 3], P('dp'), may hold values from 1 to 256, 512 in all within a row
- plan_offset: int32 [128, 128, 1], P(None, ('dp', 'ctx')), may hold values from 0 to 127, as said below
Outputs:
- mixer_out: bfloat16 [16384, 8192], P(('dp', 'ctx'))
- q_grad: bfloat16 [16384, 8192], P(('dp', 'ctx'))
- k_grad: bfloat16 [16384, 8192], P(('dp', 'ctx'))
- v_grad: bfloat16 [16384, 8192], P(('dp', 'ctx'))
- filter_grad: float32 [512, 128], P(('dp', 'ctx'))
- skip_grad: float32 [8192], P(('dp', 'ctx'))
The draws below stay inside these ranges and needn't reach their ends.
Inputs may be any that keep to these rules, and one draw needn't show every extreme that they name: For every member b, the values plan_offset[a, b, c] over all loaders a and slots c are each of 0 to 127 exactly once, and each loader's slots for b are one run of 1 row, plan_offset[a, b, c] = plan_offset[a, b, 0] + c, starting at a multiple of 1.
All inputs are finite; a program needn't handle non-finite values.
Results may differ from the reference program's by a relative error of at most 0.0056.
Values may be sent and summed in bfloat16 or wider, within the bound.
A program may use at most 320 MiB of HBM per device.

```python
import math
import jax
import jax.numpy as jnp
import numpy as np
from jax import lax

CH = 8192
FGROUPS = 512
TAPS = 128
TOK_DEV = 128
NGEN = 3
LOADERS = 128
TOKENS = 16384
GROUP_TOK = 512
CAP = 1
PER_GROUP = 16
LONGEST = 256
N_DP = 32


def draw_plan_offset(key, part):
    key = jax.random.fold_in(key, 11)
    member_keys = jax.random.split(key, LOADERS)
    starts = jax.vmap(lambda member_key: jax.random.permutation(member_key, LOADERS))(member_keys)
    slots = jnp.arange(CAP, dtype=jnp.int32)
    offsets = starts.astype(jnp.int32)[:, :, None] * CAP + slots[None, None, :]
    return offsets.transpose(1, 0, 2).astype(jnp.int32)


def with_spikes(result, rng, source, target, parts, factor):
    owner, partner = [(jnp.arange(result.shape[dim]) // (result.shape[dim] // parts)).reshape([-1 if axis == dim else 1 for axis in range(result.ndim)]) for dim in (source, target)]
    chosen = jax.random.permutation(rng, parts)[partner]
    strong = (owner == chosen) | (owner == (partner + parts // 2) % parts)
    return jnp.where(strong, factor * result, result)


def level_of(key, shape, shards, smallest, top_value):
    factor_of, own = 1.0, jax.random.fold_in(key, 6)
    for dim, blocks in shards:
        draws = jnp.exp(jax.random.uniform(jax.random.fold_in(own, dim), (blocks,), jnp.float32, smallest / len(shards), top_value / len(shards)))
        factor_of = factor_of * jnp.repeat(draws, shape[dim] // blocks).reshape([-1 if axis == dim else 1 for axis in range(len(shape))])
    return factor_of


def length_profile(count, total, bound, lean):
    weights = [(1 << 20) // math.isqrt(rank ** lean) + 1 for rank in range(2, count + 1)]
    rest, holding = total - bound - (count - 1), [1] * (count - 1)
    while rest > 0:
        candidates = [i for i in range(count - 1) if holding[i] < bound]
        whole, left = sum([weights[i] for i in candidates]), rest
        for i in candidates:
            extra = min(bound - holding[i], max(1, left * weights[i] // whole), rest)
            holding[i] = holding[i] + extra
            rest = rest - extra
    return np.array([bound] + holding)


def uneven_parts(rng, count, total, bound, lean):
    if count == 2:
        one = jax.random.randint(rng, (), max(1, total - bound), min(bound, total - 1) + 1)
        return jnp.stack([one, total - one])
    tallies = jnp.asarray(length_profile(count, total, bound, lean), jnp.int32)
    pairs = (count - 1) // 2
    giver, receiver = tallies[1:1 + 2 * pairs:2], tallies[2:2 + 2 * pairs:2]
    margin = jnp.minimum(giver - 1, bound - receiver)
    passed = jax.random.randint(jax.random.fold_in(rng, 1), (pairs,), 0, 1 << 20) % (margin + 1)
    tallies = tallies.at[1:1 + 2 * pairs:2].set(giver - passed).at[2:2 + 2 * pairs:2].set(receiver + passed)
    return tallies[jax.random.permutation(jax.random.fold_in(rng, 2), count)]


def noise(stream_key, shape, deviation, reach, cuts=(), held_as=jnp.bfloat16):
    entries = deviation * jax.random.normal(stream_key, shape, jnp.float32)
    if cuts:
        entries = entries * level_of(stream_key, shape, cuts, -0.22, 0.18)
    return jnp.clip(entries, -reach, reach).astype(held_as)


def heavy_noise(rng, dims, width, bound, shards, heavy, kind=jnp.bfloat16):
    entries = width * jax.random.normal(rng, dims, jnp.float32)
    if shards:
        entries = entries * level_of(rng, dims, shards, -0.22, 0.18)
    return jnp.clip(with_spikes(entries, jax.random.fold_in(rng, 3), *heavy), -bound, bound).astype(kind)


def setup_inputs(seed: int = 0) -> dict:
    arg_keys = jax.random.split(jax.random.key(seed), 9)
    return {
        "q_rows": noise(arg_keys[0], (TOKENS, CH), 1.0, 6.0, ((0, 128),)),
        "k_rows": noise(arg_keys[1], (TOKENS, CH), 1.0, 6.0, ((0, 128),)),
        "v_rows": noise(arg_keys[2], (TOKENS, CH), 1.0, 6.0, ((0, 128),)),
        "out_grad": heavy_noise(arg_keys[3], (TOKENS, CH), 1.0, 24.0, ((0, 128),), (0, 1, 128, 5.5)),
        "filters": noise(arg_keys[4], (FGROUPS, TAPS), TAPS ** -0.5, 0.5, (), jnp.float32),
        "skip_gain": noise(arg_keys[5], (CH,), 1.0, 4.0, (), jnp.float32),
        "genome_len": jax.vmap(lambda own: uneven_parts(own, NGEN, GROUP_TOK, LONGEST, 2))(jax.random.split(arg_keys[6], N_DP)).reshape((N_DP, NGEN)).astype(jnp.int32),
        "plan_offset": draw_plan_offset(jax.random.fold_in(arg_keys[8], 71), 0),
    }


def tap_column(coefficient, lag_index):
    return jnp.repeat(lax.dynamic_index_in_dim(coefficient, lag_index, 1, keepdims=False), PER_GROUP)

def row_pass(coefficient, skip_gain, packed):
    query_rows, mixed_rows, cotangent, segment = packed
    length = query_rows.shape[0]
    mixed_f = mixed_rows.astype(jnp.float32)
    query_f = query_rows.astype(jnp.float32)
    grad_f = cotangent.astype(jnp.float32)
    behind = jnp.concatenate([jnp.zeros((TAPS, CH), jnp.float32), mixed_f], axis=0)
    behind_seg = jnp.concatenate([jnp.full((TAPS,), -1, jnp.int32), segment.astype(jnp.int32)], axis=0)

    def forward_tap(lag_index, running):
        lag_index = jnp.asarray(lag_index).astype(jnp.int32)
        begin = (TAPS - lag_index).astype(jnp.int32)
        shifted = lax.dynamic_slice_in_dim(behind, begin, length, 0)
        shifted_seg = lax.dynamic_slice_in_dim(behind_seg, begin, length, 0)
        column = tap_column(coefficient, lag_index)
        keep = (shifted_seg == segment)[:, None]
        return running + jnp.where(keep, shifted * column[None, :], 0.0)
    filtered = lax.fori_loop(0, TAPS, forward_tap, jnp.zeros((length, CH), jnp.float32))
    gated = filtered + skip_gain[None, :] * mixed_f
    output_rows = (query_f * gated).astype(jnp.bfloat16)
    query_grad = (grad_f * gated).astype(jnp.bfloat16)
    inner = grad_f * query_f
    inner_b = lax.optimization_barrier(inner.astype(jnp.bfloat16)).astype(jnp.float32)
    ahead = jnp.concatenate([inner_b, jnp.zeros((TAPS, CH), jnp.float32)], axis=0)
    ahead_seg = jnp.concatenate([segment.astype(jnp.int32), jnp.full((TAPS,), -1, jnp.int32)], axis=0)

    def backward_tap(lag_index, carry):
        running, filter_terms = carry
        lag_index = jnp.asarray(lag_index).astype(jnp.int32)
        column = tap_column(coefficient, lag_index)
        later = lax.dynamic_slice_in_dim(ahead, lag_index, length, 0)
        later_seg = lax.dynamic_slice_in_dim(ahead_seg, lag_index, length, 0)
        running = running + jnp.where((later_seg == segment)[:, None], later * column[None, :], 0.0)
        begin = (TAPS - lag_index).astype(jnp.int32)
        shifted = lax.dynamic_slice_in_dim(behind, begin, length, 0)
        shifted_seg = lax.dynamic_slice_in_dim(behind_seg, begin, length, 0)
        product = jnp.where((shifted_seg == segment)[:, None], inner_b * shifted, 0.0)
        term = lax.optimization_barrier(jnp.sum(product.reshape(length, FGROUPS, PER_GROUP), axis=(0, 2)))
        filter_terms = lax.dynamic_update_slice(filter_terms, term[None, :], (lag_index, jnp.zeros((), jnp.int32)))
        return (running, filter_terms)
    back_conv, filter_terms = lax.fori_loop(0, TAPS, backward_tap, (jnp.zeros((length, CH), jnp.float32), jnp.zeros((TAPS, FGROUPS), jnp.float32)))
    mixed_grad = (back_conv + skip_gain[None, :] * inner).astype(jnp.bfloat16)
    skip_terms = lax.optimization_barrier(jnp.sum(inner * mixed_f, axis=0))
    return (output_rows, query_grad, mixed_grad, filter_terms, skip_terms)

def reference(q_rows, k_rows, v_rows, out_grad, filters, skip_gain, genome_len, plan_offset):
    members = jnp.arange(LOADERS, dtype=jnp.int32)
    dest = (members[None, :, None] * TOK_DEV + plan_offset.astype(jnp.int32)).reshape(-1).astype(jnp.int32)
    mixed = (k_rows.astype(jnp.float32) * v_rows.astype(jnp.float32)).astype(jnp.bfloat16)
    planned_q = jnp.zeros_like(q_rows).at[dest].set(q_rows)
    planned_u = jnp.zeros_like(mixed).at[dest].set(mixed)
    taps_b = lax.optimization_barrier(filters.astype(jnp.bfloat16))
    coefficient = taps_b.astype(jnp.float32)
    ends = jnp.cumsum(genome_len.astype(jnp.int32), axis=1).astype(jnp.int32)
    position = jnp.arange(GROUP_TOK, dtype=jnp.int32)
    genome = lax.optimization_barrier(jnp.sum((position[None, :, None] >= ends[:, None, :]).astype(jnp.int32), axis=2)).astype(jnp.int32)
    packed = (planned_q.reshape(N_DP, GROUP_TOK, CH), planned_u.reshape(N_DP, GROUP_TOK, CH), out_grad.reshape(N_DP, GROUP_TOK, CH), genome)
    output_rows, query_grad, mixed_grad, filter_terms, skip_terms = lax.map(lambda item: row_pass(coefficient, skip_gain, item), packed)
    mixer_out = output_rows.reshape(TOKENS, CH)
    q_grad = query_grad.reshape(TOKENS, CH)[dest]
    loader_mixed = mixed_grad.reshape(TOKENS, CH)[dest].astype(jnp.float32)
    k_grad = (loader_mixed * v_rows.astype(jnp.float32)).astype(jnp.bfloat16)
    v_grad = (loader_mixed * k_rows.astype(jnp.float32)).astype(jnp.bfloat16)
    filter_grad = lax.optimization_barrier(jnp.sum(filter_terms, axis=0)).T / math.sqrt(TOKENS * PER_GROUP)
    skip_grad = lax.optimization_barrier(jnp.sum(skip_terms, axis=0)) / math.sqrt(TOKENS)
    return (mixer_out, q_grad, k_grad, v_grad, filter_grad, skip_grad)
```

```python
import functools
import math

import jax
import jax.numpy as jnp
from jax import lax
from jax.experimental import pallas as pl
from jax.experimental.pallas import tpu as pltpu
from jax.sharding import PartitionSpec as P

BF = jnp.bfloat16
F32 = jnp.float32
T = 128
STEP = 16
NC = 2


def dot(a, b, dims=((1,), (0,))):
    return lax.dot_general(a, b, (dims, ((), ())), preferred_element_type=F32)


def lanes(r):
    return slice(r * T, (r + 1) * T)


def prep_kernel(q_ref, k_ref, v_ref, out_ref, sc):
    for r in range(STEP):
        sc[:, r, :] = q_ref[:, lanes(r)].astype(F32)
    out_ref[:, 0] = sc[...].astype(BF)
    for r in range(STEP):
        sc[:, r, :] = k_ref[:, lanes(r)].astype(F32) * v_ref[:, lanes(r)].astype(F32)
    out_ref[:, 1] = sc[...].astype(BF)


def prep(q, k, v, first, blocks):
    wide = pl.BlockSpec((T, STEP * T), lambda i: (0, first // STEP + i))
    return pl.pallas_call(
        prep_kernel,
        grid=(blocks // STEP,),
        in_specs=[wide] * 3,
        out_specs=pl.BlockSpec((T, 2, STEP, T), lambda i: (0, 0, i, 0)),
        out_shape=jax.ShapeDtypeStruct((T, 2, blocks, T), BF),
        scratch_shapes=[pltpu.VMEM((T, STEP, T), F32)],
        compiler_params=pltpu.CompilerParams(vmem_limit_bytes=40 * 2**20),
        name="prep",
    )(q, k, v)


def plan_kernel(got_ref, grad_ref, off_ref, q_ref, u_ref, inner_ref, sc):
    rows = lax.broadcasted_iota(jnp.int32, (T, T), 0)
    place = (rows == off_ref[...]).astype(BF)
    sc[...] = got_ref[...].astype(F32)
    for r in range(STEP):
        both = jnp.concatenate([sc[:, 0, r, :], sc[:, 1, r, :]], axis=1).astype(BF)
        planned = dot(place, both)
        q_ref[:, lanes(r)] = planned[:, :T].astype(BF)
        u_ref[:, lanes(r)] = planned[:, T:].astype(BF)
        inner_ref[:, lanes(r)] = (grad_ref[:, lanes(r)].astype(F32) * planned[:, :T]).astype(BF)


def plan(got, grad, off_row, first):
    blocks = got.shape[2]
    wide = pl.BlockSpec((T, STEP * T), lambda i: (0, i))
    there = pl.BlockSpec((T, STEP * T), lambda i: (0, first // STEP + i))
    flat = jax.ShapeDtypeStruct((T, blocks * T), BF)
    return pl.pallas_call(
        plan_kernel,
        grid=(blocks // STEP,),
        in_specs=[
            pl.BlockSpec((T, 2, STEP, T), lambda i: (0, 0, i, 0)),
            there,
            pl.BlockSpec((1, T), lambda i: (0, 0)),
        ],
        out_specs=[wide] * 3,
        out_shape=[flat] * 3,
        scratch_shapes=[pltpu.VMEM((T, 2, STEP, T), F32)],
        compiler_params=pltpu.CompilerParams(vmem_limit_bytes=40 * 2**20),
        name="plan",
    )(got, grad, off_row)


def turned(row):
    full = jnp.broadcast_to(row, (T, T))
    return pltpu.roll(full, 0, 1, stride=1, stride_axis=0)


def conv_block(u2, i2, taps, rtaps, wmask, vmask, hmask, own, flip):
    lane = lax.broadcasted_iota(jnp.int32, (1, T), 1) // 16
    f = jnp.zeros((T, T), F32)
    d = jnp.zeros((T, T), F32)
    sums = []
    inner = dot(flip, i2[:T]).astype(BF)
    for g in range(8):
        here = lane == g
        back = turned(rtaps[g : g + 1]).astype(BF)
        ahead = turned(taps[g : g + 1]).astype(BF)
        w = jnp.concatenate([back, back], axis=1) * wmask
        v = jnp.concatenate([ahead, ahead], axis=1) * vmask
        f = jnp.where(here, dot(w, u2), f)
        d = jnp.where(here, dot(v, i2), d)
        mine = jnp.where(here, inner, jnp.zeros((), BF))
        pairs = dot(mine, u2, ((1,), (1,)))
        pairs = jnp.where(own, pairs[:, T:], pairs[:, :T]) * hmask
        lags = pltpu.roll(pairs, 1, 1, stride=1, stride_axis=0)
        sums.append(jnp.sum(lags, axis=0, keepdims=True))
    return f, d, jnp.concatenate(sums, axis=0)


def conv_kernel(
    q_ref, u_ref, grad_ref, inner_ref, earlier_ref, later_ref, taps_ref, rtaps_ref, gain_ref,
    wmask_ref, vmask_ref, hmask_ref, off_ref, old_ref, out_ref, send_ref, lag_ref, skip_ref,
    dq_sc, du_sc, sc,
):
    wmask = wmask_ref[...]
    vmask = vmask_ref[...]
    hmask = hmask_ref[...]
    mirrored = lax.broadcasted_iota(jnp.int32, (T, T), 0) + lax.broadcasted_iota(jnp.int32, (T, T), 1)
    own = mirrored <= T - 1
    flip = (mirrored == T - 1).astype(BF)

    def step(n, carry):
        at = pl.ds(pl.multiple_of(n * T, T), T)
        rows = pl.ds(pl.multiple_of(n * 8, 8), 8)
        u = u_ref[:, at]
        u2 = jnp.concatenate([earlier_ref[:, at], u], axis=0)
        i2 = jnp.concatenate([inner_ref[:, at], later_ref[:, at]], axis=0)
        f, d, lags = conv_block(u2, i2, taps_ref[rows], rtaps_ref[rows], wmask, vmask, hmask, own, flip)
        lag_ref[rows, :] = lags
        gain = gain_ref[:, at]
        uf = u.astype(F32)
        qf = q_ref[:, at].astype(F32)
        gf = grad_ref[:, at].astype(F32)
        inner = gf * qf
        gated = f + gain * uf
        out_ref[:, at] = (qf * gated).astype(BF)
        dq_sc[:, at] = (gf * gated).astype(BF)
        du_sc[:, at] = (d + gain * inner).astype(BF)
        skip_ref[:, at] = jnp.sum(inner * uf, axis=0, keepdims=True)
        return carry

    lax.fori_loop(0, STEP, step, 0)
    fetch = (lax.broadcasted_iota(jnp.int32, (T, T), 1) == off_ref[...]).astype(BF)
    for r in range(STEP):
        both = jnp.concatenate([dq_sc[:, lanes(r)], du_sc[:, lanes(r)]], axis=1)
        back = dot(fetch, both)
        sc[:, 0, r, :] = back[:, :T]
        sc[:, 1, r, :] = back[:, T:]
    send_ref[...] = sc[...].astype(BF)


def conv(q, u, grad, inner, earlier, later, taps, rtaps, gain, masks, off_col, out, first):
    blocks = q.shape[1] // T
    base = first // STEP
    wide = pl.BlockSpec((T, STEP * T), lambda i: (0, i))
    there = pl.BlockSpec((T, STEP * T), lambda i: (0, base + i))
    groups = pl.BlockSpec((8 * STEP, T), lambda i: (base + i, 0))
    row = pl.BlockSpec((1, STEP * T), lambda i: (0, base + i))
    whole = lambda a: pl.BlockSpec(a.shape, lambda i: (0, 0))
    alias = {} if out is None else {13: 0}
    full = jax.ShapeDtypeStruct(grad.shape, BF)
    if out is None:
        out = jnp.zeros((8, T), BF)
    return pl.pallas_call(
        conv_kernel,
        grid=(blocks // STEP,),
        in_specs=[wide, wide, there, wide, wide, wide, groups, groups, row]
        + [whole(m) for m in masks]
        + [whole(off_col), pl.BlockSpec(memory_space=pl.ANY)],
        out_specs=[
            there,
            pl.BlockSpec((T, 2, STEP, T), lambda i: (0, 0, i, 0)),
            pl.BlockSpec((8 * STEP, T), lambda i: (i, 0)),
            pl.BlockSpec((1, STEP * T), lambda i: (0, i)),
        ],
        out_shape=[
            full,
            jax.ShapeDtypeStruct((T, 2, blocks, T), BF),
            jax.ShapeDtypeStruct((8 * blocks, T), F32),
            jax.ShapeDtypeStruct((1, blocks * T), F32),
        ],
        scratch_shapes=[
            pltpu.VMEM((T, STEP * T), BF),
            pltpu.VMEM((T, STEP * T), BF),
            pltpu.VMEM((T, 2, STEP, T), F32),
        ],
        input_output_aliases=alias,
        compiler_params=pltpu.CompilerParams(vmem_limit_bytes=48 * 2**20),
        name="conv",
    )(q, u, grad, inner, earlier, later, taps, rtaps, gain, *masks, off_col, out)


def final_kernel(got_ref, k_ref, v_ref, *rest):
    q_ref, kg_ref, vg_ref, sc = rest[-4:]
    sc[...] = got_ref[...].astype(F32)
    for r in range(STEP):
        q_ref[:, lanes(r)] = sc[:, 0, r, :].astype(BF)
        du = sc[:, 1, r, :]
        kg_ref[:, lanes(r)] = (du * v_ref[:, lanes(r)].astype(F32)).astype(BF)
        vg_ref[:, lanes(r)] = (du * k_ref[:, lanes(r)].astype(F32)).astype(BF)


def final(got, k, v, outs, first):
    blocks = got.shape[2]
    there = pl.BlockSpec((T, STEP * T), lambda i: (0, first // STEP + i))
    outs = outs or []
    return pl.pallas_call(
        final_kernel,
        grid=(blocks // STEP,),
        in_specs=[pl.BlockSpec((T, 2, STEP, T), lambda i: (0, 0, i, 0)), there, there]
        + [pl.BlockSpec(memory_space=pl.ANY)] * len(outs),
        out_specs=[there] * 3,
        out_shape=[jax.ShapeDtypeStruct(k.shape, BF)] * 3,
        scratch_shapes=[pltpu.VMEM((T, 2, STEP, T), F32)],
        input_output_aliases={3 + i: i for i in range(len(outs))},
        compiler_params=pltpu.CompilerParams(vmem_limit_bytes=40 * 2**20),
        name="final",
    )(got, k, v, *outs)


def exchange(x):
    return lax.all_to_all(x, ("dp", "ctx"), split_axis=0, concat_axis=0, tiled=True)


def masks_of(genome_len, ctx_size):
    ends = jnp.cumsum(genome_len.reshape(-1))
    start = lax.axis_index("ctx") * T
    position = start - T + jnp.arange(3 * T, dtype=jnp.int32)
    inside = (position >= 0) & (position < T * ctx_size)
    segment = jnp.sum((position[:, None] >= ends[None, :]).astype(jnp.int32), axis=1)
    segment = jnp.where(inside, segment, -1)
    before, own, after = segment[:T], segment[T : 2 * T], segment[2 * T :]
    i = jnp.arange(T, dtype=jnp.int32)[:, None]
    m = jnp.arange(T, dtype=jnp.int32)[None, :]
    same = own[:, None] == own[None, :]
    same_before = own[:, None] == before[None, :]
    same_after = own[:, None] == after[None, :]
    w_own = (m <= i) & same
    w_before = (m > i) & same_before
    wmask = jnp.concatenate([w_before, w_own], axis=1).astype(BF)
    vmask = jnp.concatenate([(m >= i) & same, (m < i) & same_after], axis=1).astype(BF)
    return wmask, vmask, (w_own | w_before).astype(F32)[::-1]


def body(q_rows, k_rows, v_rows, out_grad, filters, skip_gain, genome_len, plan_offset):
    chans = q_rows.shape[1]
    members = lax.axis_size("dp") * lax.axis_size("ctx")
    groups = filters.shape[0]
    ctx_size = lax.axis_size("ctx")
    total = members * q_rows.shape[0]
    blocks = chans // T // NC
    off_row = plan_offset.reshape(1, T)
    off_col = plan_offset.reshape(T, 1)
    masks = masks_of(genome_len, ctx_size)
    taps = filters.astype(BF).astype(F32)
    rtaps = jnp.concatenate([taps[:, :1], taps[:, :0:-1]], axis=1)
    gain = skip_gain.reshape(1, chans)
    firsts = [c * blocks for c in range(NC)]
    sent = [prep(q_rows, k_rows, v_rows, first, blocks) for first in firsts]
    got = [exchange(s) for s in sent]
    up = [(i, i + 1) for i in range(ctx_size - 1)]
    down = [(i + 1, i) for i in range(ctx_size - 1)]
    out = None
    returned, lags, skips = [], [], []
    for first, g in zip(firsts, got):
        q, u, inner = plan(g, out_grad, off_row, first)
        earlier = lax.ppermute(u, "ctx", up)
        later = lax.ppermute(inner, "ctx", down)
        out, send, lag, skip = conv(
            q, u, out_grad, inner, earlier, later, taps, rtaps, gain, masks, off_col, out, first
        )
        returned.append(exchange(send))
        lags.append(lag)
        skips.append(skip)
    lag = jnp.concatenate(lags, axis=0).reshape(members, groups // members, T)
    skip = jnp.concatenate(skips, axis=1).reshape(members, 1, chans // members)
    skip = jnp.pad(skip, ((0, 0), (0, 0), (0, T - chans // members)))
    terms = exchange(jnp.pad(jnp.concatenate([lag, skip], axis=1), ((0, 0), (0, 3), (0, 0))))
    sums = jnp.sum(terms, axis=0)
    lag_sum = sums[: groups // members]
    lag_sum = jnp.concatenate([lag_sum[:, :1], lag_sum[:, :0:-1]], axis=1)
    filter_grad = lag_sum / math.sqrt(total * (chans // groups))
    skip_grad = sums[groups // members, : chans // members] / math.sqrt(total)
    outs = None
    for first, r in zip(firsts, returned):
        outs = final(r, k_rows, v_rows, outs, first)
    return (out, *outs, filter_grad, skip_grad)


def solution(mesh):
    rows = P(("dp", "ctx"), None)
    return jax.shard_map(
        body,
        mesh=mesh,
        in_specs=(rows, rows, rows, rows, P(), P(), P("dp", None), P(None, ("dp", "ctx"), None)),
        out_specs=(rows, rows, rows, rows, rows, P(("dp", "ctx"))),
        check_vma=False,
    )
```

```python
import math

import jax
import jax.numpy as jnp
from jax import lax
from jax.experimental import pallas as pl
from jax.experimental.pallas import tpu as pltpu
from jax.sharding import PartitionSpec as P

BF = jnp.bfloat16
F32 = jnp.float32
I32 = jnp.int32
MESH = pl.DeviceIdType.MESH
T = 128
NCH = 8
LB = 8
WIDE = LB * T
GRID = (4, 4, 2, 4)
ORDERS = ("xyz", "yzx", "zxy")


def dot(a, b, dims=((1,), (0,))):
    return lax.dot_general(a, b, (dims, ((), ())), preferred_element_type=F32)


def iota(axis, shape=(T, T)):
    return lax.broadcasted_iota(I32, shape, axis)


def lanes(r):
    return slice(r * T, (r + 1) * T)


def mixer_kernel(
    q_hbm, k_hbm, v_hbm, g_hbm, taps_ref, gain_ref, len_ref, off_ref,
    out_hbm, qg_hbm, kg_hbm, vg_hbm, sum_ref,
    qv, kv, vv, gv, fa, fb, fc, fd, ba, bb, bc, bd, qp, up, ear, inn, lat,
    wmask, vmask, hmask, place, fetch, taps, rtaps, w_sc, v_sc, sc, dq_sc, du_sc,
    term, rx, ry, rz, s1, s2,
    in_sem, out_sem, fs, fr, fl, bs, br, bl, hs, hr, rs, rr,
):
    dp = lax.axis_index("dp")
    cx = lax.axis_index("ctx")
    z, y, k = dp // 8, lax.rem(dp // 2, 4), lax.rem(dp, 2)
    me = (dp, cx)
    peers = {
        "x": [(dp, lax.rem(cx + i, 4)) for i in (1, 3, 2)],
        "y": [(z * 8 + lax.rem(y + i, 4) * 2 + k, cx) for i in (1, 3, 2)],
        "z": [
            (lax.rem(z + i, 4) * 8 + y * 2 + lax.rem(k + j, 2), cx)
            for i, j in ((1, 0), (3, 0), (2, 0), (1, 1), (3, 1), (2, 1), (0, 1))
        ],
    }
    barrier = pltpu.get_barrier_semaphore()
    for axis in "xyz":
        for peer in peers[axis]:
            pl.semaphore_signal(barrier, inc=1, device_id=peer, device_id_type=MESH)

    pairs_in = ((q_hbm, qv), (k_hbm, kv), (v_hbm, vv), (g_hbm, gv))

    def cols(c):
        return slice(c * WIDE, (c + 1) * WIDE)

    def load(c, a):
        hbm, vmem = pairs_in[a]
        return pltpu.make_async_copy(hbm.at[:, cols(c)], vmem.at[:, cols(c)], in_sem.at[a, c])

    for c in range(NCH):
        for a in range(3):
            load(c, a).start()
    for c in range(NCH):
        load(c, 3).start()

    start = cx * T
    e0 = len_ref[0, 0]
    e1 = e0 + len_ref[0, 1]

    def seg(pos):
        return (pos >= e0).astype(I32) + (pos >= e1).astype(I32)

    m = iota(1)

    def same(i, which):
        own = seg(start + i)
        if which == 0:
            return own == seg(start + m)
        pos = start + which * T + m
        return (own == seg(pos)) & (pos >= 0) & (pos < 4 * T)

    i = iota(0)
    wmask[:, :T] = ((m > i) & same(i, -1)).astype(BF)
    wmask[:, T:] = ((m <= i) & same(i, 0)).astype(BF)
    vmask[:, :T] = ((m >= i) & same(i, 0)).astype(BF)
    vmask[:, T:] = ((m < i) & same(i, 1)).astype(BF)
    f = T - 1 - i
    hmask[...] = (((m > f) & same(f, -1)) | ((m <= f) & same(f, 0))).astype(F32)
    hot = (i == off_ref[...]).astype(F32)
    place[...] = hot.astype(BF)
    fetch[...] = hot.T.astype(BF)
    mirror = ((i + m == 0) | (i + m == T)).astype(BF)
    flip = (i + m == T - 1).astype(BF)
    own_side = i + m <= T - 1
    tb = taps_ref[...].astype(BF)
    taps[...] = tb.astype(F32)
    rtaps[...] = dot(tb, mirror)

    def part(buf, c, axis, dev):
        d, x = dev
        if axis == "x":
            return buf.at[c, :, :, :, x]
        if axis == "y":
            return buf.at[c, :, lax.rem(d // 2, 4)]
        return buf.at[c, d // 8, :, lax.rem(d, 2)]

    def go(bufs, sems, c, ph):
        axis = ORDERS[c % 3][ph]
        src, dst = bufs[ph], bufs[ph + 1]
        mine = pltpu.make_async_copy(
            part(src, c, axis, me), part(dst, c, axis, me), sems[2].at[c, ph]
        )
        mine.start()
        copies = [mine]
        for n, peer in enumerate(peers[axis]):
            copy = pltpu.make_async_remote_copy(
                src_ref=part(src, c, axis, peer),
                dst_ref=part(dst, c, axis, me),
                send_sem=sems[0].at[c, ph, n],
                recv_sem=sems[1].at[c, ph, n],
                device_id=peer,
                device_id_type=MESH,
            )
            copy.start()
            copies.append(copy)
        return copies

    def finish(copies):
        for copy in copies:
            copy.wait()

    fbufs, fsems = (fa, fb, fc, fd), (fs, fr, fl)
    bbufs, bsems = (ba, bb, bc, bd), (bs, br, bl)

    def rows16(value):
        return value.reshape(GRID + (16, T))

    def prep(c):
        for a in range(3):
            load(c, a).wait()
        for r in range(LB):
            at = lanes(c * LB + r)
            sc[:, r, :] = qv[:, at].astype(F32)
            sc[:, LB + r, :] = kv[:, at].astype(F32) * vv[:, at].astype(F32)
        fa[c] = rows16(sc[...].astype(BF))

    def plan(c):
        load(c, 3).wait()
        sc[...] = fd[c].reshape(T, 16, T).astype(F32)
        for r in range(LB):
            both = jnp.concatenate([sc[:, r, :], sc[:, LB + r, :]], axis=1).astype(BF)
            planned = dot(place[...], both)
            qp[c, :, lanes(r)] = planned[:, :T].astype(BF)
            up[c, :, lanes(r)] = planned[:, T:].astype(BF)
            grad = gv[:, lanes(c * LB + r)].astype(F32)
            inn[c, :, lanes(r)] = (grad * planned[:, :T]).astype(BF)

    def halo(c):
        copies = []
        for n, (src, dst, to) in enumerate(((up, ear, 0), (inn, lat, 1))):
            copy = pltpu.make_async_remote_copy(
                src_ref=src.at[c],
                dst_ref=dst.at[c],
                send_sem=hs.at[c, n],
                recv_sem=hr.at[c, n],
                device_id=peers["x"][to],
                device_id_type=MESH,
            )
            copy.start()
            copies.append(copy)
        return copies

    lane_group = iota(1, (1, T)) // 16

    def make(n, slot):
        rows = pl.ds(pl.multiple_of(n * 8, 8), 8)
        t = taps[rows]
        rt = rtaps[rows]
        for g in range(8):
            back = jnp.broadcast_to(rt[g : g + 1], (T, T))
            back = pltpu.roll(back, 0, 1, stride=1, stride_axis=0).astype(BF)
            ahead = jnp.broadcast_to(t[g : g + 1], (T, T))
            ahead = pltpu.roll(ahead, 0, 1, stride=1, stride_axis=0).astype(BF)
            w_sc[slot, lanes(g)] = jnp.concatenate([back, back], axis=1) * wmask[...]
            v_sc[slot, lanes(g)] = jnp.concatenate([ahead, ahead], axis=1) * vmask[...]

    def use(c, n, slot):
        at = pl.ds(pl.multiple_of(n * T, T), T)
        full = pl.ds(pl.multiple_of((c * LB + n) * T, T), T)
        u = up[c, :, at]
        inner_b = inn[c, :, at]
        u2 = jnp.concatenate([ear[c, :, at], u], axis=0)
        i2 = jnp.concatenate([inner_b, lat[c, :, at]], axis=0)
        f_all = dot(w_sc[slot], u2)
        d_all = dot(v_sc[slot], i2)
        turned = dot(flip, inner_b).astype(BF)
        zero = jnp.zeros((), BF)
        mine = jnp.concatenate([jnp.where(lane_group == g, turned, zero) for g in range(8)], axis=0)
        pairs = dot(mine, u2, ((1,), (1,)))
        f, d = f_all[:T], d_all[:T]
        lags = []
        for g in range(8):
            if g:
                f = jnp.where(lane_group == g, f_all[lanes(g)], f)
                d = jnp.where(lane_group == g, d_all[lanes(g)], d)
            p = pairs[lanes(g)]
            p = jnp.where(own_side, p[:, T:], p[:, :T]) * hmask[...]
            p = pltpu.roll(p, 1, 1, stride=1, stride_axis=0)
            lags.append(jnp.sum(p, axis=0, keepdims=True))
        gain = gain_ref[:, full]
        uf = u.astype(F32)
        qf = qp[c, :, at].astype(F32)
        gf = gv[:, full].astype(F32)
        inner = gf * qf
        gated = f + gain * uf
        gv[:, full] = (qf * gated).astype(BF)
        dq_sc[:, at] = (gf * gated).astype(BF)
        du_sc[:, at] = (d + gain * inner).astype(BF)
        skip = jnp.sum(inner * uf, axis=0, keepdims=True)
        other = pltpu.roll(skip, T // 2, 1)
        pad = jnp.zeros((3, T), F32)
        block = c * LB + n
        term[2 * block] = jnp.concatenate(lags[:4] + [skip, pad], axis=0)
        term[2 * block + 1] = jnp.concatenate(lags[4:] + [other, pad], axis=0)

    def conv(c):
        def step(j, carry):
            block = c * LB + 2 * j
            use(c, 2 * j, 0)
            make(block + 1, 1)
            use(c, 2 * j + 1, 1)
            make(lax.rem(block + 2, NCH * LB), 0)
            return carry

        lax.fori_loop(0, LB // 2, step, 0)
        for r in range(LB):
            both = jnp.concatenate([dq_sc[:, lanes(r)], du_sc[:, lanes(r)]], axis=1)
            back = dot(fetch[...], both)
            sc[:, r, :] = back[:, :T]
            sc[:, LB + r, :] = back[:, T:]
        ba[c] = rows16(sc[...].astype(BF))

    def store(c, a):
        vmem, hbm = ((gv, out_hbm), (qv, qg_hbm), (kv, kg_hbm), (vv, vg_hbm))[a]
        return pltpu.make_async_copy(vmem.at[:, cols(c)], hbm.at[:, cols(c)], out_sem.at[a, c])

    def last(c):
        sc[...] = bd[c].reshape(T, 16, T).astype(F32)
        for r in range(LB):
            at = lanes(c * LB + r)
            qv[:, at] = sc[:, r, :].astype(BF)
            du = sc[:, LB + r, :]
            kf = kv[:, at].astype(F32)
            vf = vv[:, at].astype(F32)
            kv[:, at] = (du * vf).astype(BF)
            vv[:, at] = (du * kf).astype(BF)
        for a in (1, 2, 3):
            store(c, a).start()

    pl.semaphore_wait(barrier, sum(len(peers[axis]) for axis in "xyz"))
    live = {}
    for c in range(NCH):
        prep(c)
        live["f", c] = go(fbufs, fsems, c, 0)
    make(0, 0)
    for ph in (1, 2):
        for c in range(NCH):
            finish(live["f", c])
            live["f", c] = go(fbufs, fsems, c, ph)
    for s in range(NCH + 5):
        if s < NCH:
            finish(live["f", s])
            plan(s)
            live["h", s] = halo(s)
        c = s - 1
        if 0 <= c < NCH:
            finish(live["h", c])
            conv(c)
            store(c, 0).start()
            live["b", c] = go(bbufs, bsems, c, 0)
        if c == NCH - 1:
            def reduce(axis, n, src, dst, peer):
                copy = pltpu.make_async_remote_copy(
                    src_ref=src, dst_ref=dst, send_sem=rs.at[n], recv_sem=rr.at[n],
                    device_id=peer, device_id_type=MESH,
                )
                copy.start()
                return copy

            grid = term.reshape(GRID + (8, T))
            live["r"] = [
                reduce("x", n, grid.at[:, :, :, p[1]], rx.at[n], p)
                for n, p in enumerate(peers["x"])
            ]
        for back, ph in ((2, 1), (3, 2)):
            b = s - back
            if 0 <= b < NCH:
                finish(live["b", b])
                live["b", b] = go(bbufs, bsems, b, ph)
        if s == NCH + 1:
            finish(live["r"])
            s1[...] = grid[:, :, :, cx] + rx[0] + rx[1] + rx[2]
            live["r"] = [
                reduce("y", 3 + n, s1.at[:, lax.rem(p[0] // 2, 4)], ry.at[n], p)
                for n, p in enumerate(peers["y"])
            ]
        if s == NCH + 2:
            finish(live["r"])
            s2[...] = s1[:, y] + ry[0] + ry[1] + ry[2]
            live["r"] = [
                reduce("z", 6 + n, s2.at[p[0] // 8, lax.rem(p[0], 2)], rz.at[n], p)
                for n, p in enumerate(peers["z"])
            ]
        if s == NCH + 3:
            finish(live["r"])
            total = s2[z, k]
            for n in range(7):
                total = total + rz[n]
            hi = total.astype(BF)
            rest = total - hi.astype(F32)
            mid = rest.astype(BF)
            low = (rest - mid.astype(F32)).astype(BF)
            turned = dot(hi, mirror) + dot(mid, mirror) + dot(low, mirror)
            row = iota(0, (8, T))
            tokens = T * T
            sum_ref[...] = jnp.where(
                row < 4, turned * (1 / math.sqrt(tokens * 16)), total * (1 / math.sqrt(tokens))
            )
        c = s - 4
        if 0 <= c < NCH:
            finish(live["b", c])
            last(c)
    for c in range(NCH):
        for a in range(4):
            store(c, a).wait()


def body(q_rows, k_rows, v_rows, out_grad, filters, skip_gain, genome_len, plan_offset):
    chans = q_rows.shape[1]
    wide = (T, chans)
    act = jax.ShapeDtypeStruct(wide, BF)
    anywhere = pl.BlockSpec(memory_space=pl.ANY)
    vmem = pl.BlockSpec(memory_space=pltpu.VMEM)
    smem = pl.BlockSpec(memory_space=pltpu.SMEM)
    flow = pltpu.VMEM((NCH,) + GRID + (16, T), BF)
    chunked = pltpu.VMEM((NCH, T, WIDE), BF)
    dma = pltpu.SemaphoreType.DMA
    groups = filters.shape[0]
    *outs, sums = pl.pallas_call(
        mixer_kernel,
        in_specs=[anywhere] * 4 + [vmem, vmem, smem, vmem],
        out_specs=[anywhere] * 4 + [vmem],
        out_shape=[act] * 4 + [jax.ShapeDtypeStruct((8, T), F32)],
        scratch_shapes=[pltpu.VMEM(wide, BF)] * 4
        + [flow] * 8
        + [chunked] * 5
        + [
            pltpu.VMEM((T, 2 * T), BF),
            pltpu.VMEM((T, 2 * T), BF),
            pltpu.VMEM((T, T), F32),
            pltpu.VMEM((T, T), BF),
            pltpu.VMEM((T, T), BF),
            pltpu.VMEM((groups, T), F32),
            pltpu.VMEM((groups, T), F32),
            pltpu.VMEM((2, 8 * T, 2 * T), BF),
            pltpu.VMEM((2, 8 * T, 2 * T), BF),
            pltpu.VMEM((T, 16, T), F32),
            pltpu.VMEM((T, WIDE), BF),
            pltpu.VMEM((T, WIDE), BF),
            pltpu.VMEM((T, 8, T), F32),
            pltpu.VMEM((3, 4, 4, 2, 8, T), F32),
            pltpu.VMEM((3, 4, 2, 8, T), F32),
            pltpu.VMEM((7, 8, T), F32),
            pltpu.VMEM((4, 4, 2, 8, T), F32),
            pltpu.VMEM((4, 2, 8, T), F32),
            dma((4, NCH)),
            dma((4, NCH)),
            dma((NCH, 3, 7)),
            dma((NCH, 3, 7)),
            dma((NCH, 3)),
            dma((NCH, 3, 7)),
            dma((NCH, 3, 7)),
            dma((NCH, 3)),
            dma((NCH, 2)),
            dma((NCH, 2)),
            dma((13,)),
            dma((13,)),
        ],
        compiler_params=pltpu.CompilerParams(
            collective_id=0, has_side_effects=True, vmem_limit_bytes=60 * 2**20
        ),
        name="mixer",
    )(
        q_rows, k_rows, v_rows, out_grad, filters, skip_gain.reshape(1, chans), genome_len,
        plan_offset.reshape(1, T),
    )
    return (*outs, sums[:4], sums[4, : chans // T])


def solution(mesh):
    rows = P(("dp", "ctx"), None)
    return jax.shard_map(
        body,
        mesh=mesh,
        in_specs=(rows, rows, rows, rows, P(), P(), P("dp", None), P(None, ("dp", "ctx"), None)),
        out_specs=(rows, rows, rows, rows, rows, P(("dp", "ctx"))),
        check_vma=False,
    )
```

```python
import math

import jax
import jax.numpy as jnp
from jax import lax
from jax.experimental import pallas as pl
from jax.experimental.pallas import tpu as pltpu
from jax.sharding import PartitionSpec as P

BF = jnp.bfloat16
F32 = jnp.float32
I32 = jnp.int32
MESH = pl.DeviceIdType.MESH
T = 128
NCH = 8
LB = 8
WIDE = LB * T
GRID = (4, 4, 2, 4)
PREP, PLAN, CONV, LAST, MOVE_THERE, MOVE_BACK, MOVE_TERMS = range(7)
ORDERS_THERE = ("xzy", "yxz", "yzx", "xyz", "xzy", "xyz", "yxz", "yxz")
ORDERS_BACK = ("zyx", "zxy", "zxy", "zyx", "yzx", "zyx", "zxy", "zyx")
SCHEDULE = (
    0, 400, 0, 410, 0, 420, 0, 430, 401, 411, 0, 440, 0, 450, 421, 431, 402, 0, 460, 412, 422,
    441, 432, 451, 403, 100, 442, 0, 470, 461, 413, 100, 423, 100, 452, 200, 500, 433, 100, 471,
    443, 100, 200, 510, 501, 453, 100, 462, 200, 520, 200, 530, 463, 100, 472, 502, 200, 540, 521,
    200, 550, 531, 473, 100, 200, 560, 511, 551, 532, 522, 541, 200, 570, 600, 561, 503, 300, 601,
    512, 552, 602, 542, 571, 603, 513, 300, 523, 300, 533, 300, 562, 572, 543, 300, 553, 300, 563,
    300, 573, 300,
)


def dot(a, b, dims=((1,), (0,))):
    return lax.dot_general(a, b, (dims, ((), ())), preferred_element_type=F32)


def iota(axis, shape=(T, T)):
    return lax.broadcasted_iota(I32, shape, axis)


def lanes(r):
    return slice(r * T, (r + 1) * T)


def mixer_kernel(
    q_hbm, k_hbm, v_hbm, g_hbm, taps_ref, gain_ref, len_ref, off_ref,
    out_hbm, qg_hbm, kg_hbm, vg_hbm, sum_ref,
    qv, kv, vv, gv, fa, fb, fc, fd, ba, bb, bc, bd, qp, up, ear, inn, lat,
    wmask, vmask, hmask, place, fetch, taps, rtaps, w_sc, v_sc, sc, dq_sc, du_sc,
    term, rx, ry, rz, s1, s2,
    in_sem, out_sem, fs, fr, fl, bs, br, bl, hs, hr, rs, rr,
):
    dp = lax.axis_index("dp")
    cx = lax.axis_index("ctx")
    z, y, k = dp // 8, lax.rem(dp // 2, 4), lax.rem(dp, 2)
    me = (dp, cx)
    peers = {
        "x": [(dp, lax.rem(cx + i, 4)) for i in (1, 3, 2)],
        "y": [(z * 8 + lax.rem(y + i, 4) * 2 + k, cx) for i in (1, 3, 2)],
        "z": [
            (lax.rem(z + i, 4) * 8 + y * 2 + lax.rem(k + j, 2), cx)
            for i, j in ((1, 0), (3, 0), (2, 0), (1, 1), (3, 1), (2, 1), (0, 1))
        ],
    }
    barrier = pltpu.get_barrier_semaphore()
    for axis in "xyz":
        for peer in peers[axis]:
            pl.semaphore_signal(barrier, inc=1, device_id=peer, device_id_type=MESH)

    pairs_in = ((q_hbm, qv), (k_hbm, kv), (v_hbm, vv), (g_hbm, gv))

    def cols(c):
        return pl.ds(pl.multiple_of(c * WIDE, WIDE), WIDE)

    def block_of(c, r):
        return pl.ds(pl.multiple_of((c * LB + r) * T, T), T)

    def load(c, a):
        hbm, vmem = pairs_in[a]
        return pltpu.make_async_copy(hbm.at[:, cols(c)], vmem.at[:, cols(c)], in_sem.at[a, c])

    for c in range(NCH):
        for a in range(3):
            load(c, a).start()
    for c in range(NCH):
        load(c, 3).start()

    start = cx * T
    e0 = len_ref[0, 0]
    e1 = e0 + len_ref[0, 1]

    def seg(pos):
        return (pos >= e0).astype(I32) + (pos >= e1).astype(I32)

    m = iota(1)

    def same(i, which):
        own = seg(start + i)
        if which == 0:
            return own == seg(start + m)
        pos = start + which * T + m
        return (own == seg(pos)) & (pos >= 0) & (pos < 4 * T)

    i = iota(0)
    wmask[:, :T] = ((m > i) & same(i, -1)).astype(BF)
    wmask[:, T:] = ((m <= i) & same(i, 0)).astype(BF)
    vmask[:, :T] = ((m >= i) & same(i, 0)).astype(BF)
    vmask[:, T:] = ((m < i) & same(i, 1)).astype(BF)
    f = T - 1 - i
    hmask[...] = (((m > f) & same(f, -1)) | ((m <= f) & same(f, 0))).astype(F32)
    hot = (i == off_ref[...]).astype(F32)
    place[...] = hot.astype(BF)
    fetch[...] = hot.T.astype(BF)
    mirror = ((i + m == 0) | (i + m == T)).astype(BF)
    flip = (i + m == T - 1).astype(BF)
    own_side = i + m <= T - 1
    tb = taps_ref[...].astype(BF)
    taps[...] = tb.astype(F32)
    rtaps[...] = dot(tb, mirror)

    def part(buf, c, axis, dev):
        d, x = dev
        if axis == "x":
            return buf.at[c, :, :, :, x]
        if axis == "y":
            return buf.at[c, :, lax.rem(d // 2, 4)]
        return buf.at[c, d // 8, :, lax.rem(d, 2)]

    def moves(bufs, sems, orders, c, ph):
        axis = orders[c][ph]
        src, dst = bufs[ph], bufs[ph + 1]
        copies = [
            pltpu.make_async_copy(
                part(src, c, axis, me), part(dst, c, axis, me), sems[2].at[c, ph]
            )
        ]
        for n, peer in enumerate(peers[axis]):
            copies.append(
                pltpu.make_async_remote_copy(
                    src_ref=part(src, c, axis, peer),
                    dst_ref=part(dst, c, axis, me),
                    send_sem=sems[0].at[c, ph, n],
                    recv_sem=sems[1].at[c, ph, n],
                    device_id=peer,
                    device_id_type=MESH,
                )
            )
        return copies

    def begin(copies):
        for copy in copies:
            copy.start()

    def finish(copies):
        for copy in copies:
            copy.wait()

    there = ((fa, fb, fc, fd), (fs, fr, fl), ORDERS_THERE)
    back_way = ((ba, bb, bc, bd), (bs, br, bl), ORDERS_BACK)

    def rows16(value):
        return value.reshape(GRID + (16, T))

    def prep(c):
        for a in range(3):
            load(c, a).wait()
        for r in range(LB):
            at = block_of(c, r)
            sc[:, r, :] = qv[:, at].astype(F32)
            sc[:, LB + r, :] = kv[:, at].astype(F32) * vv[:, at].astype(F32)
        fa[c] = rows16(sc[...].astype(BF))

    def plan(c):
        load(c, 3).wait()
        sc[...] = fd[c].reshape(T, 16, T).astype(F32)
        for r in range(LB):
            both = jnp.concatenate([sc[:, r, :], sc[:, LB + r, :]], axis=1).astype(BF)
            planned = dot(place[...], both)
            qp[c, :, lanes(r)] = planned[:, :T].astype(BF)
            up[c, :, lanes(r)] = planned[:, T:].astype(BF)
            grad = gv[:, block_of(c, r)].astype(F32)
            inn[c, :, lanes(r)] = (grad * planned[:, :T]).astype(BF)

    def halo(c):
        copies = []
        for n, (src, dst, to) in enumerate(((up, ear, 0), (inn, lat, 1))):
            copy = pltpu.make_async_remote_copy(
                src_ref=src.at[c],
                dst_ref=dst.at[c],
                send_sem=hs.at[c, n],
                recv_sem=hr.at[c, n],
                device_id=peers["x"][to],
                device_id_type=MESH,
            )
            copies.append(copy)
        return copies

    lane_group = iota(1, (1, T)) // 16

    def make(n, slot):
        rows = pl.ds(pl.multiple_of(n * 8, 8), 8)
        t = taps[rows]
        rt = rtaps[rows]
        for g in range(8):
            back = jnp.broadcast_to(rt[g : g + 1], (T, T))
            back = pltpu.roll(back, 0, 1, stride=1, stride_axis=0).astype(BF)
            ahead = jnp.broadcast_to(t[g : g + 1], (T, T))
            ahead = pltpu.roll(ahead, 0, 1, stride=1, stride_axis=0).astype(BF)
            w_sc[slot, lanes(g)] = jnp.concatenate([back, back], axis=1) * wmask[...]
            v_sc[slot, lanes(g)] = jnp.concatenate([ahead, ahead], axis=1) * vmask[...]

    def use(c, n, slot):
        at = pl.ds(pl.multiple_of(n * T, T), T)
        full = pl.ds(pl.multiple_of((c * LB + n) * T, T), T)
        u = up[c, :, at]
        inner_b = inn[c, :, at]
        u2 = jnp.concatenate([ear[c, :, at], u], axis=0)
        i2 = jnp.concatenate([inner_b, lat[c, :, at]], axis=0)
        f_all = dot(w_sc[slot], u2)
        d_all = dot(v_sc[slot], i2)
        turned = dot(flip, inner_b).astype(BF)
        zero = jnp.zeros((), BF)
        mine = jnp.concatenate([jnp.where(lane_group == g, turned, zero) for g in range(8)], axis=0)
        pairs = dot(mine, u2, ((1,), (1,)))
        f, d = f_all[:T], d_all[:T]
        lags = []
        for g in range(8):
            if g:
                f = jnp.where(lane_group == g, f_all[lanes(g)], f)
                d = jnp.where(lane_group == g, d_all[lanes(g)], d)
            p = pairs[lanes(g)]
            p = jnp.where(own_side, p[:, T:], p[:, :T]) * hmask[...]
            p = pltpu.roll(p, 1, 1, stride=1, stride_axis=0)
            lags.append(jnp.sum(p, axis=0, keepdims=True))
        gain = gain_ref[:, full]
        uf = u.astype(F32)
        qf = qp[c, :, at].astype(F32)
        gf = gv[:, full].astype(F32)
        inner = gf * qf
        gated = f + gain * uf
        gv[:, full] = (qf * gated).astype(BF)
        dq_sc[:, at] = (gf * gated).astype(BF)
        du_sc[:, at] = (d + gain * inner).astype(BF)
        skip = jnp.sum(inner * uf, axis=0, keepdims=True)
        other = pltpu.roll(skip, T // 2, 1)
        pad = jnp.zeros((3, T), F32)
        block = c * LB + n
        term[2 * block] = jnp.concatenate(lags[:4] + [skip, pad], axis=0)
        term[2 * block + 1] = jnp.concatenate(lags[4:] + [other, pad], axis=0)

    def conv(c):
        def step(j, carry):
            block = c * LB + 2 * j
            use(c, 2 * j, 0)
            make(block + 1, 1)
            use(c, 2 * j + 1, 1)
            make(lax.rem(block + 2, NCH * LB), 0)
            return carry

        lax.fori_loop(0, LB // 2, step, 0)
        for r in range(LB):
            both = jnp.concatenate([dq_sc[:, lanes(r)], du_sc[:, lanes(r)]], axis=1)
            back = dot(fetch[...], both)
            sc[:, r, :] = back[:, :T]
            sc[:, LB + r, :] = back[:, T:]
        ba[c] = rows16(sc[...].astype(BF))

    def store(c, a):
        vmem, hbm = ((gv, out_hbm), (qv, qg_hbm), (kv, kg_hbm), (vv, vg_hbm))[a]
        return pltpu.make_async_copy(vmem.at[:, cols(c)], hbm.at[:, cols(c)], out_sem.at[a, c])

    def last(c):
        sc[...] = bd[c].reshape(T, 16, T).astype(F32)
        for r in range(LB):
            at = block_of(c, r)
            qv[:, at] = sc[:, r, :].astype(BF)
            du = sc[:, LB + r, :]
            kf = kv[:, at].astype(F32)
            vf = vv[:, at].astype(F32)
            kv[:, at] = (du * vf).astype(BF)
            vv[:, at] = (du * kf).astype(BF)
        for a in (1, 2, 3):
            store(c, a).start()

    grid = term.reshape(GRID + (8, T))

    def term_moves(axis):
        view, slots, base = {
            "x": (lambda p: grid.at[:, :, :, p[1]], rx, 0),
            "y": (lambda p: s1.at[:, lax.rem(p[0] // 2, 4)], ry, 3),
            "z": (lambda p: s2.at[p[0] // 8, lax.rem(p[0], 2)], rz, 6),
        }[axis]
        return [
            pltpu.make_async_remote_copy(
                src_ref=view(peer), dst_ref=slots.at[n], send_sem=rs.at[base + n],
                recv_sem=rr.at[base + n], device_id=peer, device_id_type=MESH,
            )
            for n, peer in enumerate(peers[axis])
        ]

    def reduce(stage):
        if stage == 0:
            begin(term_moves("x"))
        elif stage == 1:
            finish(term_moves("x"))
            s1[...] = grid[:, :, :, cx] + rx[0] + rx[1] + rx[2]
            begin(term_moves("y"))
        elif stage == 2:
            finish(term_moves("y"))
            s2[...] = s1[:, y] + ry[0] + ry[1] + ry[2]
            begin(term_moves("z"))
        else:
            finish(term_moves("z"))
            total = s2[z, k]
            for n in range(7):
                total = total + rz[n]
            hi = total.astype(BF)
            rest = total - hi.astype(F32)
            mid = rest.astype(BF)
            low = (rest - mid.astype(F32)).astype(BF)
            turned = dot(hi, mirror) + dot(mid, mirror) + dot(low, mirror)
            row = iota(0, (8, T))
            tokens = T * T
            sum_ref[...] = jnp.where(
                row < 4, turned * (1 / math.sqrt(tokens * 16)), total * (1 / math.sqrt(tokens))
            )

    def move(code):
        kind, c, ph = code // 100, code // 10 % 10, code % 10
        if kind == MOVE_TERMS:
            reduce(ph)
            return
        way = there if kind == MOVE_THERE else back_way
        if ph:
            finish(moves(*way, c, ph - 1))
        if ph < 3:
            begin(moves(*way, c, ph))

    def work(kind, c):
        if kind == PREP:
            prep(c)
        elif kind == PLAN:
            plan(c)
            begin(halo(c))
        elif kind == CONV:
            finish(halo(c))
            conv(c)
            store(c, 0).start()
        else:
            last(c)

    steps = [([], None)]
    for code in SCHEDULE:
        if code < 400:
            steps[-1] = (steps[-1][0], code // 100)
            steps.append(([], None))
        else:
            steps[-1][0].append(code)
    tail = steps.pop()[0]

    def choose(i, low, high):
        if not any(steps[n][0] for n in range(low, high)):
            return
        if high - low == 1:
            for code in steps[low][0]:
                move(code)
            return
        mid = (low + high) // 2
        pl.when(i < mid)(lambda: choose(i, low, mid))
        pl.when(i >= mid)(lambda: choose(i, mid, high))

    words = [
        sum(steps[n][1] << (2 * (n - first)) for n in range(first, min(first + 12, len(steps))))
        for first in range(0, len(steps), 12)
    ]

    def step(i, counts):
        choose(i, 0, len(steps))
        word = jnp.asarray(words[0], I32)
        for n in range(1, len(words)):
            word = jnp.where(i >= 12 * n, words[n], word)
        kind = lax.rem(lax.shift_right_logical(word, 2 * lax.rem(i, 12)), 4)
        for n in range(4):
            pl.when(kind == n)(lambda n=n: work(n, counts[n]))
        return tuple(counts[n] + (kind == n).astype(I32) for n in range(4))

    pl.semaphore_wait(barrier, sum(len(peers[axis]) for axis in "xyz"))
    make(0, 0)
    zero_count = jnp.zeros((), I32)
    lax.fori_loop(0, len(steps), step, (zero_count,) * 4)
    for code in tail:
        move(code)
    for c in range(NCH):
        for a in range(4):
            store(c, a).wait()


def body(q_rows, k_rows, v_rows, out_grad, filters, skip_gain, genome_len, plan_offset):
    chans = q_rows.shape[1]
    wide = (T, chans)
    act = jax.ShapeDtypeStruct(wide, BF)
    anywhere = pl.BlockSpec(memory_space=pl.ANY)
    vmem = pl.BlockSpec(memory_space=pltpu.VMEM)
    smem = pl.BlockSpec(memory_space=pltpu.SMEM)
    flow = pltpu.VMEM((NCH,) + GRID + (16, T), BF)
    chunked = pltpu.VMEM((NCH, T, WIDE), BF)
    dma = pltpu.SemaphoreType.DMA
    groups = filters.shape[0]
    *outs, sums = pl.pallas_call(
        mixer_kernel,
        in_specs=[anywhere] * 4 + [vmem, vmem, smem, vmem],
        out_specs=[anywhere] * 4 + [vmem],
        out_shape=[act] * 4 + [jax.ShapeDtypeStruct((8, T), F32)],
        scratch_shapes=[pltpu.VMEM(wide, BF)] * 4
        + [flow] * 8
        + [chunked] * 5
        + [
            pltpu.VMEM((T, 2 * T), BF),
            pltpu.VMEM((T, 2 * T), BF),
            pltpu.VMEM((T, T), F32),
            pltpu.VMEM((T, T), BF),
            pltpu.VMEM((T, T), BF),
            pltpu.VMEM((groups, T), F32),
            pltpu.VMEM((groups, T), F32),
            pltpu.VMEM((2, 8 * T, 2 * T), BF),
            pltpu.VMEM((2, 8 * T, 2 * T), BF),
            pltpu.VMEM((T, 16, T), F32),
            pltpu.VMEM((T, WIDE), BF),
            pltpu.VMEM((T, WIDE), BF),
            pltpu.VMEM((T, 8, T), F32),
            pltpu.VMEM((3, 4, 4, 2, 8, T), F32),
            pltpu.VMEM((3, 4, 2, 8, T), F32),
            pltpu.VMEM((7, 8, T), F32),
            pltpu.VMEM((4, 4, 2, 8, T), F32),
            pltpu.VMEM((4, 2, 8, T), F32),
            dma((4, NCH)),
            dma((4, NCH)),
            dma((NCH, 3, 7)),
            dma((NCH, 3, 7)),
            dma((NCH, 3)),
            dma((NCH, 3, 7)),
            dma((NCH, 3, 7)),
            dma((NCH, 3)),
            dma((NCH, 2)),
            dma((NCH, 2)),
            dma((13,)),
            dma((13,)),
        ],
        compiler_params=pltpu.CompilerParams(
            collective_id=0, has_side_effects=True, vmem_limit_bytes=60 * 2**20
        ),
        name="mixer",
    )(
        q_rows, k_rows, v_rows, out_grad, filters, skip_gain.reshape(1, chans), genome_len,
        plan_offset.reshape(1, T),
    )
    return (*outs, sums[:4], sums[4, : chans // T])


def solution(mesh):
    rows = P(("dp", "ctx"), None)
    return jax.shard_map(
        body,
        mesh=mesh,
        in_specs=(rows, rows, rows, rows, P(), P(), P("dp", None), P(None, ("dp", "ctx"), None)),
        out_specs=(rows, rows, rows, rows, rows, P(("dp", "ctx"))),
        check_vma=False,
    )
```

```python
import math

import jax
import jax.numpy as jnp
from jax import lax
from jax.experimental import pallas as pl
from jax.experimental.pallas import tpu as pltpu
from jax.sharding import PartitionSpec as P

BF = jnp.bfloat16
F32 = jnp.float32
I32 = jnp.int32
MESH = pl.DeviceIdType.MESH
T = 128
NCH = 8
LB = 8
WIDE = LB * T
GRID = (4, 4, 2, 4)
PREP, PLAN, CONV, LAST, MOVE_THERE, MOVE_BACK, MOVE_TERMS, SET_UP = range(8)
ORDERS_THERE = ("xzy", "yxz", "yzx", "xyz", "xzy", "xyz", "yxz", "yxz")
ORDERS_BACK = ("zyx", "zxy", "zxy", "zyx", "yzx", "zyx", "zxy", "zyx")
SCHEDULE = (
    0, 400, 0, 410, 0, 420, 700, 0, 430, 401, 411, 0, 440, 0, 450, 421, 431, 402, 0, 460, 412,
    422, 441, 432, 451, 403, 100, 442, 0, 470, 461, 413, 100, 423, 100, 452, 200, 500, 433, 100,
    471, 443, 100, 200, 510, 501, 453, 100, 462, 200, 520, 200, 530, 463, 100, 472, 502, 200, 540,
    521, 200, 550, 531, 473, 100, 200, 560, 511, 551, 532, 522, 541, 200, 570, 600, 561, 503, 300,
    601, 512, 552, 602, 542, 571, 603, 513, 300, 523, 300, 533, 300, 562, 572, 543, 300, 553, 300,
    563, 300, 573, 300,
)


def dot(a, b, dims=((1,), (0,))):
    return lax.dot_general(a, b, (dims, ((), ())), preferred_element_type=F32)


def iota(axis, shape=(T, T)):
    return lax.broadcasted_iota(I32, shape, axis)


def lanes(r):
    return slice(r * T, (r + 1) * T)


def mixer_kernel(
    q_hbm, k_hbm, v_hbm, g_hbm, taps_ref, gain_ref, len_ref, off_ref,
    gv, qv, kv, vv, filter_ref, skip_ref,
    fa, fb, fc, fd, ba, bb, bc, bd, qp, up, ear, inn, lat,
    wmask, vmask, hmask, place, fetch, taps, rtaps, w_sc, v_sc, sc, dq_sc, du_sc,
    term, rx, ry, rz, s1, s2,
    in_sem, fs, fr, fl, bs, br, bl, hs, hr, rs, rr,
):
    dp = lax.axis_index("dp")
    cx = lax.axis_index("ctx")
    z, y, k = dp // 8, lax.rem(dp // 2, 4), lax.rem(dp, 2)
    me = (dp, cx)
    peers = {
        "x": [(dp, lax.rem(cx + i, 4)) for i in (1, 3, 2)],
        "y": [(z * 8 + lax.rem(y + i, 4) * 2 + k, cx) for i in (1, 3, 2)],
        "z": [
            (lax.rem(z + i, 4) * 8 + y * 2 + lax.rem(k + j, 2), cx)
            for i, j in ((1, 0), (3, 0), (2, 0), (1, 1), (3, 1), (2, 1), (0, 1))
        ],
    }
    barrier = pltpu.get_barrier_semaphore()
    for axis in "xyz":
        for peer in peers[axis]:
            pl.semaphore_signal(barrier, inc=1, device_id=peer, device_id_type=MESH)

    pairs_in = ((q_hbm, qv), (k_hbm, kv), (v_hbm, vv), (g_hbm, gv))

    def cols(c):
        return pl.ds(pl.multiple_of(c * WIDE, WIDE), WIDE)

    def block_of(c, r):
        return pl.ds(pl.multiple_of((c * LB + r) * T, T), T)

    def load(c, a):
        hbm, vmem = pairs_in[a]
        return pltpu.make_async_copy(hbm.at[:, cols(c)], vmem.at[:, cols(c)], in_sem.at[a, c])

    for c in range(NCH):
        for a in range(3):
            load(c, a).start()
    for c in range(NCH):
        load(c, 3).start()

    i = iota(0)
    m = iota(1)
    mirror = ((i + m == 0) | (i + m == T)).astype(BF)
    flip = (i + m == T - 1).astype(BF)
    own_side = i + m <= T - 1

    def set_up():
        start = cx * T
        e0 = len_ref[0, 0]
        e1 = e0 + len_ref[0, 1]

        def seg(pos):
            return (pos >= e0).astype(I32) + (pos >= e1).astype(I32)

        def same(i, which):
            own = seg(start + i)
            if which == 0:
                return own == seg(start + m)
            pos = start + which * T + m
            return (own == seg(pos)) & (pos >= 0) & (pos < 4 * T)

        wmask[:, :T] = ((m > i) & same(i, -1)).astype(BF)
        wmask[:, T:] = ((m <= i) & same(i, 0)).astype(BF)
        vmask[:, :T] = ((m >= i) & same(i, 0)).astype(BF)
        vmask[:, T:] = ((m < i) & same(i, 1)).astype(BF)
        f = T - 1 - i
        hmask[...] = (((m > f) & same(f, -1)) | ((m <= f) & same(f, 0))).astype(F32)
        hot = (i == off_ref[...]).astype(F32)
        place[...] = hot.astype(BF)
        fetch[...] = hot.T.astype(BF)
        tb = taps_ref[...].astype(BF)
        taps[...] = tb.astype(F32)
        rtaps[...] = dot(tb, mirror)

    def part(buf, c, axis, dev):
        d, x = dev
        if axis == "x":
            return buf.at[c, :, :, :, x]
        if axis == "y":
            return buf.at[c, :, lax.rem(d // 2, 4)]
        return buf.at[c, d // 8, :, lax.rem(d, 2)]

    def moves(bufs, sems, orders, c, ph):
        axis = orders[c][ph]
        src, dst = bufs[ph], bufs[ph + 1]
        copies = [
            pltpu.make_async_copy(
                part(src, c, axis, me), part(dst, c, axis, me), sems[2].at[c, ph]
            )
        ]
        for n, peer in enumerate(peers[axis]):
            copies.append(
                pltpu.make_async_remote_copy(
                    src_ref=part(src, c, axis, peer),
                    dst_ref=part(dst, c, axis, me),
                    send_sem=sems[0].at[c, ph, n],
                    recv_sem=sems[1].at[c, ph, n],
                    device_id=peer,
                    device_id_type=MESH,
                )
            )
        return copies

    def begin(copies):
        for copy in copies:
            copy.start()

    def finish(copies):
        for copy in copies:
            copy.wait()

    there = ((fa, fb, fc, fd), (fs, fr, fl), ORDERS_THERE)
    back_way = ((ba, bb, bc, bd), (bs, br, bl), ORDERS_BACK)

    def rows16(value):
        return value.reshape(GRID + (16, T))

    def prep(c):
        for a in range(3):
            load(c, a).wait()
        for r in range(LB):
            at = block_of(c, r)
            sc[:, r, :] = qv[:, at].astype(F32)
            sc[:, LB + r, :] = kv[:, at].astype(F32) * vv[:, at].astype(F32)
        fa[c] = rows16(sc[...].astype(BF))

    def plan(c):
        load(c, 3).wait()
        sc[...] = fd[c].reshape(T, 16, T).astype(F32)
        for r in range(LB):
            both = jnp.concatenate([sc[:, r, :], sc[:, LB + r, :]], axis=1).astype(BF)
            planned = dot(place[...], both)
            qp[c, :, lanes(r)] = planned[:, :T].astype(BF)
            up[c, :, lanes(r)] = planned[:, T:].astype(BF)
            grad = gv[:, block_of(c, r)].astype(F32)
            inn[c, :, lanes(r)] = (grad * planned[:, :T]).astype(BF)

    def halo(c):
        copies = []
        for n, (src, dst, to) in enumerate(((up, ear, 0), (inn, lat, 1))):
            copy = pltpu.make_async_remote_copy(
                src_ref=src.at[c],
                dst_ref=dst.at[c],
                send_sem=hs.at[c, n],
                recv_sem=hr.at[c, n],
                device_id=peers["x"][to],
                device_id_type=MESH,
            )
            copies.append(copy)
        return copies

    lane_group = iota(1, (1, T)) // 16

    def make(n, slot):
        rows = pl.ds(pl.multiple_of(n * 8, 8), 8)
        t = taps[rows]
        rt = rtaps[rows]
        for g in range(8):
            back = jnp.broadcast_to(rt[g : g + 1], (T, T))
            back = pltpu.roll(back, 0, 1, stride=1, stride_axis=0).astype(BF)
            ahead = jnp.broadcast_to(t[g : g + 1], (T, T))
            ahead = pltpu.roll(ahead, 0, 1, stride=1, stride_axis=0).astype(BF)
            w_sc[slot, lanes(g)] = jnp.concatenate([back, back], axis=1) * wmask[...]
            v_sc[slot, lanes(g)] = jnp.concatenate([ahead, ahead], axis=1) * vmask[...]

    def use(c, n, slot):
        at = pl.ds(pl.multiple_of(n * T, T), T)
        full = pl.ds(pl.multiple_of((c * LB + n) * T, T), T)
        u = up[c, :, at]
        inner_b = inn[c, :, at]
        u2 = jnp.concatenate([ear[c, :, at], u], axis=0)
        i2 = jnp.concatenate([inner_b, lat[c, :, at]], axis=0)
        f_all = dot(w_sc[slot], u2)
        d_all = dot(v_sc[slot], i2)
        turned = dot(flip, inner_b).astype(BF)
        zero = jnp.zeros((), BF)
        mine = jnp.concatenate([jnp.where(lane_group == g, turned, zero) for g in range(8)], axis=0)
        pairs = dot(mine, u2, ((1,), (1,)))
        f, d = f_all[:T], d_all[:T]
        lags = []
        for g in range(8):
            if g:
                f = jnp.where(lane_group == g, f_all[lanes(g)], f)
                d = jnp.where(lane_group == g, d_all[lanes(g)], d)
            p = pairs[lanes(g)]
            p = jnp.where(own_side, p[:, T:], p[:, :T]) * hmask[...]
            p = pltpu.roll(p, 1, 1, stride=1, stride_axis=0)
            lags.append(jnp.sum(p, axis=0, keepdims=True))
        gain = gain_ref[:, full]
        uf = u.astype(F32)
        qf = qp[c, :, at].astype(F32)
        gf = gv[:, full].astype(F32)
        inner = gf * qf
        gated = f + gain * uf
        gv[:, full] = (qf * gated).astype(BF)
        dq_sc[:, at] = (gf * gated).astype(BF)
        du_sc[:, at] = (d + gain * inner).astype(BF)
        skip = jnp.sum(inner * uf, axis=0, keepdims=True)
        other = pltpu.roll(skip, T // 2, 1)
        pad = jnp.zeros((3, T), F32)
        block = c * LB + n
        term[2 * block] = jnp.concatenate(lags[:4] + [skip, pad], axis=0)
        term[2 * block + 1] = jnp.concatenate(lags[4:] + [other, pad], axis=0)

    def conv(c):
        def step(j, carry):
            block = c * LB + 2 * j
            use(c, 2 * j, 0)
            make(block + 1, 1)
            use(c, 2 * j + 1, 1)
            make(lax.rem(block + 2, NCH * LB), 0)
            return carry

        lax.fori_loop(0, LB // 2, step, 0)
        for r in range(LB):
            both = jnp.concatenate([dq_sc[:, lanes(r)], du_sc[:, lanes(r)]], axis=1)
            back = dot(fetch[...], both)
            sc[:, r, :] = back[:, :T]
            sc[:, LB + r, :] = back[:, T:]
        ba[c] = rows16(sc[...].astype(BF))

    def last(c):
        sc[...] = bd[c].reshape(T, 16, T).astype(F32)
        for r in range(LB):
            at = block_of(c, r)
            qv[:, at] = sc[:, r, :].astype(BF)
            du = sc[:, LB + r, :]
            kf = kv[:, at].astype(F32)
            vf = vv[:, at].astype(F32)
            kv[:, at] = (du * vf).astype(BF)
            vv[:, at] = (du * kf).astype(BF)

    grid = term.reshape(GRID + (8, T))

    def term_moves(axis):
        view, slots, base = {
            "y": (lambda p: grid.at[:, lax.rem(p[0] // 2, 4)], ry, 0),
            "z": (lambda p: s1.at[p[0] // 8, lax.rem(p[0], 2)], rz, 3),
            "x": (lambda p: s2.at[p[1]], rx, 10),
        }[axis]
        return [
            pltpu.make_async_remote_copy(
                src_ref=view(peer), dst_ref=slots.at[n], send_sem=rs.at[base + n],
                recv_sem=rr.at[base + n], device_id=peer, device_id_type=MESH,
            )
            for n, peer in enumerate(peers[axis])
        ]

    def reduce(stage):
        if stage == 0:
            begin(term_moves("y"))
        elif stage == 1:
            finish(term_moves("y"))
            s1[...] = grid[:, y] + ry[0] + ry[1] + ry[2]
            begin(term_moves("z"))
        elif stage == 2:
            finish(term_moves("z"))
            total = s1[z, k]
            for n in range(7):
                total = total + rz[n]
            s2[...] = total
            begin(term_moves("x"))
        else:
            finish(term_moves("x"))
            total = s2[cx] + rx[0] + rx[1] + rx[2]
            hi = total.astype(BF)
            rest = total - hi.astype(F32)
            mid = rest.astype(BF)
            low = (rest - mid.astype(F32)).astype(BF)
            turned = dot(hi, mirror) + dot(mid, mirror) + dot(low, mirror)
            tokens = T * T
            filter_ref[...] = turned[:4] * (1 / math.sqrt(tokens * 16))
            skip_ref[...] = total[4:5, :64] * (1 / math.sqrt(tokens))

    def move(code):
        kind, c, ph = code // 100, code // 10 % 10, code % 10
        if kind == SET_UP:
            set_up()
            make(0, 0)
            return
        if kind == MOVE_TERMS:
            reduce(ph)
            return
        way = there if kind == MOVE_THERE else back_way
        if ph:
            finish(moves(*way, c, ph - 1))
        if ph < 3:
            begin(moves(*way, c, ph))

    def work(kind, c):
        if kind == PREP:
            prep(c)
        elif kind == PLAN:
            plan(c)
            begin(halo(c))
        elif kind == CONV:
            finish(halo(c))
            conv(c)
        else:
            last(c)

    steps = [([], None)]
    for code in SCHEDULE:
        if code < 400:
            steps[-1] = (steps[-1][0], code // 100)
            steps.append(([], None))
        else:
            steps[-1][0].append(code)
    tail = steps.pop()[0]

    def choose(i, low, high):
        if not any(steps[n][0] for n in range(low, high)):
            return
        if high - low == 1:
            for code in steps[low][0]:
                move(code)
            return
        mid = (low + high) // 2
        pl.when(i < mid)(lambda: choose(i, low, mid))
        pl.when(i >= mid)(lambda: choose(i, mid, high))

    words = [
        sum(steps[n][1] << (2 * (n - first)) for n in range(first, min(first + 12, len(steps))))
        for first in range(0, len(steps), 12)
    ]

    def step(i, counts):
        choose(i, 0, len(steps))
        word = jnp.asarray(words[0], I32)
        for n in range(1, len(words)):
            word = jnp.where(i >= 12 * n, words[n], word)
        kind = lax.rem(lax.shift_right_logical(word, 2 * lax.rem(i, 12)), 4)
        for n in range(4):
            pl.when(kind == n)(lambda n=n: work(n, counts[n]))
        return tuple(counts[n] + (kind == n).astype(I32) for n in range(4))

    pl.semaphore_wait(barrier, sum(len(peers[axis]) for axis in "xyz"))
    zero_count = jnp.zeros((), I32)
    lax.fori_loop(0, len(steps), step, (zero_count,) * 4)
    for code in tail:
        move(code)


def body(q_rows, k_rows, v_rows, out_grad, filters, skip_gain, genome_len, plan_offset):
    chans = q_rows.shape[1]
    wide = (T, chans)
    act = pltpu.VMEM(wide, BF)
    anywhere = pl.BlockSpec(memory_space=pl.ANY)
    vmem = pl.BlockSpec(memory_space=pltpu.VMEM)
    smem = pl.BlockSpec(memory_space=pltpu.SMEM)
    flow = pltpu.VMEM((NCH,) + GRID + (16, T), BF)
    chunked = pltpu.VMEM((NCH, T, WIDE), BF)
    dma = pltpu.SemaphoreType.DMA
    groups = filters.shape[0]
    *outs, filter_grad, skip_grad = pl.pallas_call(
        mixer_kernel,
        in_specs=[anywhere] * 4 + [vmem, vmem, smem, vmem],
        out_specs=[vmem] * 6,
        out_shape=[act] * 4
        + [
            jax.ShapeDtypeStruct((groups // T, T), F32),
            jax.ShapeDtypeStruct((1, chans // T), F32),
        ],
        scratch_shapes=[flow] * 8
        + [chunked] * 5
        + [
            pltpu.VMEM((T, 2 * T), BF),
            pltpu.VMEM((T, 2 * T), BF),
            pltpu.VMEM((T, T), F32),
            pltpu.VMEM((T, T), BF),
            pltpu.VMEM((T, T), BF),
            pltpu.VMEM((groups, T), F32),
            pltpu.VMEM((groups, T), F32),
            pltpu.VMEM((2, 8 * T, 2 * T), BF),
            pltpu.VMEM((2, 8 * T, 2 * T), BF),
            pltpu.VMEM((T, 16, T), F32),
            pltpu.VMEM((T, WIDE), BF),
            pltpu.VMEM((T, WIDE), BF),
            pltpu.VMEM((T, 8, T), F32),
            pltpu.VMEM((3, 8, T), F32),
            pltpu.VMEM((3, 4, 2, 4, 8, T), F32),
            pltpu.VMEM((7, 4, 8, T), F32),
            pltpu.VMEM((4, 2, 4, 8, T), F32),
            pltpu.VMEM((4, 8, T), F32),
            dma((4, NCH)),
            dma((NCH, 3, 7)),
            dma((NCH, 3, 7)),
            dma((NCH, 3)),
            dma((NCH, 3, 7)),
            dma((NCH, 3, 7)),
            dma((NCH, 3)),
            dma((NCH, 2)),
            dma((NCH, 2)),
            dma((13,)),
            dma((13,)),
        ],
        compiler_params=pltpu.CompilerParams(
            collective_id=0, has_side_effects=True, vmem_limit_bytes=52 * 2**20
        ),
        name="mixer",
    )(
        q_rows, k_rows, v_rows, out_grad, filters, skip_gain.reshape(1, chans), genome_len,
        plan_offset.reshape(1, T),
    )
    return (*outs, filter_grad, skip_grad.reshape(chans // T))


def solution(mesh):
    rows = P(("dp", "ctx"), None)
    return jax.shard_map(
        body,
        mesh=mesh,
        in_specs=(rows, rows, rows, rows, P(), P(), P("dp", None), P(None, ("dp", "ctx"), None)),
        out_specs=(rows, rows, rows, rows, rows, P(("dp", "ctx"))),
        check_vma=False,
    )
```

```python
import math

import jax
import jax.numpy as jnp
from jax import lax
from jax.experimental import pallas as pl
from jax.experimental.pallas import tpu as pltpu
from jax.sharding import PartitionSpec as P

BF = jnp.bfloat16
F32 = jnp.float32
I32 = jnp.int32
MESH = pl.DeviceIdType.MESH
T = 128
NCH = 8
LB = 8
WIDE = LB * T
GRID = (4, 4, 2, 4)
PREP, PLAN, CONV, LAST, MOVE_THERE, MOVE_BACK, MOVE_TERMS, SET_UP = range(8)
ORDERS_THERE = ("xzy", "yxz", "yzx", "xyz", "xzy", "xyz", "yxz", "yxz")
ORDERS_BACK = ("zyx", "zxy", "zxy", "zyx", "yzx", "zyx", "zxy", "zyx")
SCHEDULE = (
    0, 400, 700, 0, 410, 0, 420, 710, 0, 430, 401, 411, 0, 440, 0, 450, 421, 431, 402, 0, 460,
    412, 422, 441, 432, 451, 403, 100, 442, 0, 470, 461, 413, 100, 423, 100, 452, 200, 500, 433,
    100, 471, 443, 100, 200, 510, 501, 453, 100, 462, 200, 520, 200, 530, 463, 100, 472, 502, 200,
    540, 521, 200, 550, 531, 473, 100, 200, 560, 511, 551, 532, 522, 541, 200, 570, 600, 561, 503,
    300, 601, 512, 552, 602, 542, 571, 603, 513, 300, 523, 300, 533, 300, 562, 572, 543, 300, 553,
    300, 563, 300, 573, 300,
)


def dot(a, b, dims=((1,), (0,))):
    return lax.dot_general(a, b, (dims, ((), ())), preferred_element_type=F32)


def iota(axis, shape=(T, T)):
    return lax.broadcasted_iota(I32, shape, axis)


def lanes(r):
    return slice(r * T, (r + 1) * T)


def mixer_kernel(
    q_hbm, k_hbm, v_hbm, g_hbm, taps_ref, gain_ref, len_ref, off_ref,
    gv, qv, kv, vv, filter_ref, skip_ref,
    fa, fb, fc, fd, ba, bb, bc, bd, qp, up, ear, inn, lat,
    wmask, vmask, hmask, place, fetch, taps, rtaps, w_sc, v_sc, sc, dq_sc, du_sc,
    term, rx, ry, rz, s1, s2,
    in_sem, fs, fr, fl, bs, br, bl, hs, hr, rs, rr,
):
    dp = lax.axis_index("dp")
    cx = lax.axis_index("ctx")
    z, y, k = dp // 8, lax.rem(dp // 2, 4), lax.rem(dp, 2)
    me = (dp, cx)
    peers = {
        "x": [(dp, lax.rem(cx + i, 4)) for i in (1, 3, 2)],
        "y": [(z * 8 + lax.rem(y + i, 4) * 2 + k, cx) for i in (1, 3, 2)],
        "z": [
            (lax.rem(z + i, 4) * 8 + y * 2 + lax.rem(k + j, 2), cx)
            for i, j in ((1, 0), (3, 0), (2, 0), (1, 1), (3, 1), (2, 1), (0, 1))
        ],
    }

    pairs_in = ((q_hbm, qv), (k_hbm, kv), (v_hbm, vv), (g_hbm, gv))

    def cols(c):
        return pl.ds(pl.multiple_of(c * WIDE, WIDE), WIDE)

    def block_of(c, r):
        return pl.ds(pl.multiple_of((c * LB + r) * T, T), T)

    def load(c, a):
        hbm, vmem = pairs_in[a]
        return pltpu.make_async_copy(hbm.at[:, cols(c)], vmem.at[:, cols(c)], in_sem.at[a, c])


    i = iota(0)
    m = iota(1)
    mirror = ((i + m == 0) | (i + m == T)).astype(BF)
    flip = (i + m == T - 1).astype(BF)
    own_side = i + m <= T - 1

    def set_up():
        start = cx * T
        e0 = len_ref[0, 0]
        e1 = e0 + len_ref[0, 1]

        def seg(pos):
            return (pos >= e0).astype(I32) + (pos >= e1).astype(I32)

        def same(i, which):
            own = seg(start + i)
            if which == 0:
                return own == seg(start + m)
            pos = start + which * T + m
            return (own == seg(pos)) & (pos >= 0) & (pos < 4 * T)

        wmask[:, :T] = ((m > i) & same(i, -1)).astype(BF)
        wmask[:, T:] = ((m <= i) & same(i, 0)).astype(BF)
        vmask[:, :T] = ((m >= i) & same(i, 0)).astype(BF)
        vmask[:, T:] = ((m < i) & same(i, 1)).astype(BF)
        f = T - 1 - i
        hmask[...] = (((m > f) & same(f, -1)) | ((m <= f) & same(f, 0))).astype(F32)
        hot = (i == off_ref[...]).astype(F32)
        place[...] = hot.astype(BF)
        fetch[...] = hot.T.astype(BF)
        tb = taps_ref[...].astype(BF)
        taps[...] = tb.astype(F32)
        rtaps[...] = dot(tb, mirror)

    for a in range(3):
        load(0, a).start()
    barrier = pltpu.get_barrier_semaphore()
    for axis in "xyz":
        for peer in peers[axis]:
            pl.semaphore_signal(barrier, inc=1, device_id=peer, device_id_type=MESH)
    for a in range(3):
        load(1, a).start()

    def load_rest():
        for c in range(2, NCH):
            for a in range(3):
                load(c, a).start()
        for c in range(NCH):
            load(c, 3).start()

    def part(buf, c, axis, dev):
        d, x = dev
        if axis == "x":
            return buf.at[c, x]
        if axis == "y":
            return buf.at[c, :, :, :, lax.rem(d // 2, 4)]
        return buf.at[c, :, d // 8, lax.rem(d, 2)]

    def moves(bufs, sems, orders, c, ph):
        axis = orders[c][ph]
        src, dst = bufs[ph], bufs[ph + 1]
        copies = [
            pltpu.make_async_copy(
                part(src, c, axis, me), part(dst, c, axis, me), sems[2].at[c, ph]
            )
        ]
        for n, peer in enumerate(peers[axis]):
            copies.append(
                pltpu.make_async_remote_copy(
                    src_ref=part(src, c, axis, peer),
                    dst_ref=part(dst, c, axis, me),
                    send_sem=sems[0].at[c, ph, n],
                    recv_sem=sems[1].at[c, ph, n],
                    device_id=peer,
                    device_id_type=MESH,
                )
            )
        return copies

    def begin(copies):
        for copy in copies:
            copy.start()

    def finish(copies):
        for copy in copies:
            copy.wait()

    there = ((fa, fb, fc, fd), (fs, fr, fl), ORDERS_THERE)
    back_way = ((ba, bb, bc, bd), (bs, br, bl), ORDERS_BACK)

    by_grid = sc.reshape(GRID + (16, T))

    def pack(buf, c):
        for k in range(2):
            for x in range(4):
                buf[c, x, :, k] = by_grid[:, :, k, x].astype(BF)

    def unpack(buf, c):
        for k in range(2):
            for x in range(4):
                by_grid[:, :, k, x] = buf[c, x, :, k].astype(F32)

    def prep(c):
        for a in range(3):
            load(c, a).wait()
        for r in range(LB):
            at = block_of(c, r)
            sc[:, r, :] = qv[:, at].astype(F32)
            sc[:, LB + r, :] = kv[:, at].astype(F32) * vv[:, at].astype(F32)
        pack(fa, c)

    def plan(c):
        load(c, 3).wait()
        unpack(fd, c)
        for r in range(LB):
            both = jnp.concatenate([sc[:, r, :], sc[:, LB + r, :]], axis=1).astype(BF)
            planned = dot(place[...], both)
            qp[c, :, lanes(r)] = planned[:, :T].astype(BF)
            up[c, :, lanes(r)] = planned[:, T:].astype(BF)
            grad = gv[:, block_of(c, r)].astype(F32)
            inn[c, :, lanes(r)] = (grad * planned[:, :T]).astype(BF)

    def halo(c):
        copies = []
        for n, (src, dst, to) in enumerate(((up, ear, 0), (inn, lat, 1))):
            copy = pltpu.make_async_remote_copy(
                src_ref=src.at[c],
                dst_ref=dst.at[c],
                send_sem=hs.at[c, n],
                recv_sem=hr.at[c, n],
                device_id=peers["x"][to],
                device_id_type=MESH,
            )
            copies.append(copy)
        return copies

    lane_group = iota(1, (1, T)) // 16

    def make(n, slot):
        rows = pl.ds(pl.multiple_of(n * 8, 8), 8)
        t = taps[rows]
        rt = rtaps[rows]
        for g in range(8):
            back = jnp.broadcast_to(rt[g : g + 1], (T, T))
            back = pltpu.roll(back, 0, 1, stride=1, stride_axis=0).astype(BF)
            ahead = jnp.broadcast_to(t[g : g + 1], (T, T))
            ahead = pltpu.roll(ahead, 0, 1, stride=1, stride_axis=0).astype(BF)
            w_sc[slot, lanes(g)] = jnp.concatenate([back, back], axis=1) * wmask[...]
            v_sc[slot, lanes(g)] = jnp.concatenate([ahead, ahead], axis=1) * vmask[...]

    def use(c, n, slot):
        at = pl.ds(pl.multiple_of(n * T, T), T)
        full = pl.ds(pl.multiple_of((c * LB + n) * T, T), T)
        u = up[c, :, at]
        inner_b = inn[c, :, at]
        u2 = jnp.concatenate([ear[c, :, at], u], axis=0)
        i2 = jnp.concatenate([inner_b, lat[c, :, at]], axis=0)
        f_all = dot(w_sc[slot], u2)
        d_all = dot(v_sc[slot], i2)
        turned = dot(flip, inner_b).astype(BF)
        zero = jnp.zeros((), BF)
        mine = jnp.concatenate([jnp.where(lane_group == g, turned, zero) for g in range(8)], axis=0)
        pairs = dot(mine, u2, ((1,), (1,)))
        f, d = f_all[:T], d_all[:T]
        lags = []
        for g in range(8):
            if g:
                f = jnp.where(lane_group == g, f_all[lanes(g)], f)
                d = jnp.where(lane_group == g, d_all[lanes(g)], d)
            p = pairs[lanes(g)]
            p = jnp.where(own_side, p[:, T:], p[:, :T]) * hmask[...]
            p = pltpu.roll(p, 1, 1, stride=1, stride_axis=0)
            lags.append(jnp.sum(p, axis=0, keepdims=True))
        gain = gain_ref[:, full]
        uf = u.astype(F32)
        qf = qp[c, :, at].astype(F32)
        gf = gv[:, full].astype(F32)
        inner = gf * qf
        gated = f + gain * uf
        gv[:, full] = (qf * gated).astype(BF)
        dq_sc[:, at] = (gf * gated).astype(BF)
        du_sc[:, at] = (d + gain * inner).astype(BF)
        skip = jnp.sum(inner * uf, axis=0, keepdims=True)
        other = pltpu.roll(skip, T // 2, 1)
        pad = jnp.zeros((3, T), F32)
        block = c * LB + n
        term[2 * block] = jnp.concatenate(lags[:4] + [skip, pad], axis=0)
        term[2 * block + 1] = jnp.concatenate(lags[4:] + [other, pad], axis=0)

    def conv(c):
        def step(j, carry):
            block = c * LB + 2 * j
            use(c, 2 * j, 0)
            make(block + 1, 1)
            use(c, 2 * j + 1, 1)
            make(lax.rem(block + 2, NCH * LB), 0)
            return carry

        lax.fori_loop(0, LB // 2, step, 0)
        for r in range(LB):
            both = jnp.concatenate([dq_sc[:, lanes(r)], du_sc[:, lanes(r)]], axis=1)
            back = dot(fetch[...], both)
            sc[:, r, :] = back[:, :T]
            sc[:, LB + r, :] = back[:, T:]
        pack(ba, c)

    def last(c):
        unpack(bd, c)
        for r in range(LB):
            at = block_of(c, r)
            qv[:, at] = sc[:, r, :].astype(BF)
            du = sc[:, LB + r, :]
            kf = kv[:, at].astype(F32)
            vf = vv[:, at].astype(F32)
            kv[:, at] = (du * vf).astype(BF)
            vv[:, at] = (du * kf).astype(BF)

    grid = term.reshape(GRID + (8, T))

    def term_moves(axis):
        view, slots, base = {
            "y": (lambda p: grid.at[:, lax.rem(p[0] // 2, 4)], ry, 0),
            "z": (lambda p: s1.at[p[0] // 8, lax.rem(p[0], 2)], rz, 3),
            "x": (lambda p: s2.at[p[1]], rx, 10),
        }[axis]
        return [
            pltpu.make_async_remote_copy(
                src_ref=view(peer), dst_ref=slots.at[n], send_sem=rs.at[base + n],
                recv_sem=rr.at[base + n], device_id=peer, device_id_type=MESH,
            )
            for n, peer in enumerate(peers[axis])
        ]

    def reduce(stage):
        if stage == 0:
            begin(term_moves("y"))
        elif stage == 1:
            finish(term_moves("y"))
            s1[...] = grid[:, y] + ry[0] + ry[1] + ry[2]
            begin(term_moves("z"))
        elif stage == 2:
            finish(term_moves("z"))
            total = s1[z, k]
            for n in range(7):
                total = total + rz[n]
            s2[...] = total
            begin(term_moves("x"))
        else:
            finish(term_moves("x"))
            total = s2[cx] + rx[0] + rx[1] + rx[2]
            hi = total.astype(BF)
            rest = total - hi.astype(F32)
            mid = rest.astype(BF)
            low = (rest - mid.astype(F32)).astype(BF)
            turned = dot(hi, mirror) + dot(mid, mirror) + dot(low, mirror)
            tokens = T * T
            filter_ref[...] = turned[:4] * (1 / math.sqrt(tokens * 16))
            skip_ref[...] = total[4:5, :64] * (1 / math.sqrt(tokens))

    def move(code):
        kind, c, ph = code // 100, code // 10 % 10, code % 10
        if kind == SET_UP and not c:
            load_rest()
            return
        if kind == SET_UP:
            set_up()
            make(0, 0)
            return
        if kind == MOVE_TERMS:
            reduce(ph)
            return
        way = there if kind == MOVE_THERE else back_way
        if ph:
            finish(moves(*way, c, ph - 1))
        if ph < 3:
            begin(moves(*way, c, ph))

    def work(kind, c):
        if kind == PREP:
            prep(c)
        elif kind == PLAN:
            plan(c)
            begin(halo(c))
        elif kind == CONV:
            finish(halo(c))
            conv(c)
        else:
            last(c)

    steps = [([], None)]
    for code in SCHEDULE:
        if code < 400:
            steps[-1] = (steps[-1][0], code // 100)
            steps.append(([], None))
        else:
            steps[-1][0].append(code)
    tail = steps.pop()[0]

    def choose(i, low, high):
        if not any(steps[n][0] for n in range(low, high)):
            return
        if high - low == 1:
            for code in steps[low][0]:
                move(code)
            return
        mid = (low + high) // 2
        pl.when(i < mid)(lambda: choose(i, low, mid))
        pl.when(i >= mid)(lambda: choose(i, mid, high))

    words = [
        sum(steps[n][1] << (2 * (n - first)) for n in range(first, min(first + 12, len(steps))))
        for first in range(0, len(steps), 12)
    ]

    def step(i, counts):
        choose(i, 0, len(steps))
        word = jnp.asarray(words[0], I32)
        for n in range(1, len(words)):
            word = jnp.where(i >= 12 * n, words[n], word)
        kind = lax.rem(lax.shift_right_logical(word, 2 * lax.rem(i, 12)), 4)
        for n in range(4):
            pl.when(kind == n)(lambda n=n: work(n, counts[n]))
        return tuple(counts[n] + (kind == n).astype(I32) for n in range(4))

    pl.semaphore_wait(barrier, sum(len(peers[axis]) for axis in "xyz"))
    zero_count = jnp.zeros((), I32)
    lax.fori_loop(0, len(steps), step, (zero_count,) * 4)
    for code in tail:
        move(code)


def hand_out(*refs):
    n = 6
    ins, outs, sems = refs[:n], refs[n : 2 * n], refs[-1]
    copies = []
    for a in range(4):
        for part in range(4):
            rows = pl.ds(part * 32, 32)
            copies.append(
                pltpu.make_async_copy(ins[a].at[rows], outs[a].at[rows], sems.at[a, part])
            )
    for copy in copies:
        copy.start()
    outs[4][...] = ins[4][...]
    outs[5][...] = ins[5][...]
    for copy in copies:
        copy.wait()


def body(q_rows, k_rows, v_rows, out_grad, filters, skip_gain, genome_len, plan_offset):
    chans = q_rows.shape[1]
    wide = (T, chans)
    act = pltpu.VMEM(wide, BF)
    anywhere = pl.BlockSpec(memory_space=pl.ANY)
    vmem = pl.BlockSpec(memory_space=pltpu.VMEM)
    smem = pl.BlockSpec(memory_space=pltpu.SMEM)
    flow = pltpu.VMEM((NCH, 4, 4, 2, 4, 16, T), BF)
    chunked = pltpu.VMEM((NCH, T, WIDE), BF)
    dma = pltpu.SemaphoreType.DMA
    groups = filters.shape[0]
    results = pl.pallas_call(
        mixer_kernel,
        in_specs=[anywhere] * 4 + [vmem, vmem, smem, vmem],
        out_specs=[vmem] * 6,
        out_shape=[act] * 4
        + [
            pltpu.VMEM((groups // T, T), F32),
            pltpu.VMEM((1, chans // T), F32),
        ],
        scratch_shapes=[flow] * 8
        + [chunked] * 5
        + [
            pltpu.VMEM((T, 2 * T), BF),
            pltpu.VMEM((T, 2 * T), BF),
            pltpu.VMEM((T, T), F32),
            pltpu.VMEM((T, T), BF),
            pltpu.VMEM((T, T), BF),
            pltpu.VMEM((groups, T), F32),
            pltpu.VMEM((groups, T), F32),
            pltpu.VMEM((2, 8 * T, 2 * T), BF),
            pltpu.VMEM((2, 8 * T, 2 * T), BF),
            pltpu.VMEM((T, 16, T), F32),
            pltpu.VMEM((T, WIDE), BF),
            pltpu.VMEM((T, WIDE), BF),
            pltpu.VMEM((T, 8, T), F32),
            pltpu.VMEM((3, 8, T), F32),
            pltpu.VMEM((3, 4, 2, 4, 8, T), F32),
            pltpu.VMEM((7, 4, 8, T), F32),
            pltpu.VMEM((4, 2, 4, 8, T), F32),
            pltpu.VMEM((4, 8, T), F32),
            dma((4, NCH)),
            dma((NCH, 3, 7)),
            dma((NCH, 3, 7)),
            dma((NCH, 3)),
            dma((NCH, 3, 7)),
            dma((NCH, 3, 7)),
            dma((NCH, 3)),
            dma((NCH, 2)),
            dma((NCH, 2)),
            dma((13,)),
            dma((13,)),
        ],
        compiler_params=pltpu.CompilerParams(
            collective_id=0, has_side_effects=True, vmem_limit_bytes=52 * 2**20
        ),
        name="mixer",
    )(
        q_rows, k_rows, v_rows, out_grad, filters, skip_gain.reshape(1, chans), genome_len,
        plan_offset.reshape(1, T),
    )
    *outs, skip_grad = pl.pallas_call(
        hand_out,
        in_specs=[vmem] * 6,
        out_specs=[anywhere] * 4 + [vmem] * 2,
        out_shape=[jax.ShapeDtypeStruct(r.shape, r.dtype) for r in results],
        scratch_shapes=[dma((4, 4))],
        compiler_params=pltpu.CompilerParams(vmem_limit_bytes=2 * 2**20),
        name="hand_out",
    )(*[pltpu.with_memory_space_constraint(r, pltpu.VMEM) for r in results])
    return (*outs, skip_grad.reshape(chans // T))


def solution(mesh):
    rows = P(("dp", "ctx"), None)
    return jax.shard_map(
        body,
        mesh=mesh,
        in_specs=(rows, rows, rows, rows, P(), P(), P("dp", None), P(None, ("dp", "ctx"), None)),
        out_specs=(rows, rows, rows, rows, rows, P(("dp", "ctx"))),
        check_vma=False,
    )
```

```python
import math

import jax
import jax.numpy as jnp
from jax import lax
from jax.experimental import pallas as pl
from jax.experimental.pallas import tpu as pltpu
from jax.sharding import PartitionSpec as P

BF = jnp.bfloat16
F32 = jnp.float32
I32 = jnp.int32
MESH = pl.DeviceIdType.MESH
T = 128
NCH = 8
LB = 8
WIDE = LB * T
GRID = (4, 4, 2, 4)
PREP, PLAN, CONV, LAST, MOVE_THERE, MOVE_BACK, MOVE_TERMS, SET_UP = range(8)
ORDERS_THERE = ("xzy", "yxz", "yzx", "xyz", "xzy", "xyz", "yxz", "yxz")
ORDERS_BACK = ("zyx", "zxy", "zxy", "zyx", "yzx", "zyx", "zxy", "zyx")
SCHEDULE = (
    0, 400, 700, 0, 410, 0, 420, 710, 0, 430, 401, 411, 0, 440, 0, 450, 421, 431, 402, 0, 460,
    412, 422, 441, 432, 451, 403, 100, 442, 0, 470, 461, 413, 100, 423, 100, 452, 200, 500, 433,
    100, 471, 443, 100, 200, 510, 501, 453, 100, 462, 200, 520, 200, 530, 463, 100, 472, 502, 200,
    540, 521, 200, 550, 531, 473, 100, 200, 560, 511, 551, 532, 522, 541, 200, 570, 600, 561, 503,
    300, 601, 512, 552, 602, 542, 571, 603, 513, 300, 523, 300, 533, 300, 562, 572, 543, 300, 553,
    300, 563, 300, 573, 300,
)


def dot(a, b, dims=((1,), (0,))):
    return lax.dot_general(a, b, (dims, ((), ())), preferred_element_type=F32)


def iota(axis, shape=(T, T)):
    return lax.broadcasted_iota(I32, shape, axis)


def lanes(r):
    return slice(r * T, (r + 1) * T)


def mixer_kernel(
    q_hbm, k_hbm, v_hbm, g_hbm, taps_ref, gain_ref, len_ref, off_ref,
    gv, qv, kv, vv, filter_ref, skip_ref,
    fa, fb, fc, fd, ba, bb, bc, bd, qp, up, ear, inn, lat,
    wmask, vmask, hmask, place, fetch, taps, rtaps, w_sc, v_sc, sc, dq_sc, du_sc,
    term, rx, ry, rz, s1, s2,
    in_sem, fs, fr, fl, bs, br, bl, hs, hr, rs, rr,
):
    dp = lax.axis_index("dp")
    cx = lax.axis_index("ctx")
    z, y, k = dp // 8, lax.rem(dp // 2, 4), lax.rem(dp, 2)
    me = (dp, cx)
    peers = {
        "x": [(dp, lax.rem(cx + i, 4)) for i in (2, 1, 3)],
        "y": [(z * 8 + lax.rem(y + i, 4) * 2 + k, cx) for i in (2, 1, 3)],
        "z": [
            (lax.rem(z + i, 4) * 8 + y * 2 + lax.rem(k + j, 2), cx)
            for i, j in ((2, 0), (2, 1), (1, 0), (3, 0), (1, 1), (3, 1), (0, 1))
        ],
    }

    pairs_in = ((q_hbm, qv), (k_hbm, kv), (v_hbm, vv), (g_hbm, gv))

    def cols(c):
        return pl.ds(pl.multiple_of(c * WIDE, WIDE), WIDE)

    def block_of(c, r):
        return pl.ds(pl.multiple_of((c * LB + r) * T, T), T)

    def load(c, a):
        hbm, vmem = pairs_in[a]
        return pltpu.make_async_copy(hbm.at[:, cols(c)], vmem.at[:, cols(c)], in_sem.at[a, c])


    i = iota(0)
    m = iota(1)
    mirror = ((i + m == 0) | (i + m == T)).astype(BF)
    flip = (i + m == T - 1).astype(BF)
    own_side = i + m <= T - 1

    def set_up():
        start = cx * T
        e0 = len_ref[0, 0]
        e1 = e0 + len_ref[0, 1]

        def seg(pos):
            return (pos >= e0).astype(I32) + (pos >= e1).astype(I32)

        def same(i, which):
            own = seg(start + i)
            if which == 0:
                return own == seg(start + m)
            pos = start + which * T + m
            return (own == seg(pos)) & (pos >= 0) & (pos < 4 * T)

        wmask[:, :T] = ((m > i) & same(i, -1)).astype(BF)
        wmask[:, T:] = ((m <= i) & same(i, 0)).astype(BF)
        vmask[:, :T] = ((m >= i) & same(i, 0)).astype(BF)
        vmask[:, T:] = ((m < i) & same(i, 1)).astype(BF)
        f = T - 1 - i
        hmask[...] = (((m > f) & same(f, -1)) | ((m <= f) & same(f, 0))).astype(F32)
        hot = (i == off_ref[...]).astype(F32)
        place[...] = hot.astype(BF)
        fetch[...] = hot.T.astype(BF)
        tb = taps_ref[...].astype(BF)
        taps[...] = tb.astype(F32)
        rtaps[...] = dot(tb, mirror)

    for a in range(3):
        load(0, a).start()
    barrier = pltpu.get_barrier_semaphore()
    for axis in "xyz":
        for peer in peers[axis]:
            pl.semaphore_signal(barrier, inc=1, device_id=peer, device_id_type=MESH)
    for a in range(3):
        load(1, a).start()

    def load_rest():
        for c in range(2, NCH):
            for a in range(3):
                load(c, a).start()
        for c in range(NCH):
            load(c, 3).start()

    def part(buf, c, axis, dev):
        d, x = dev
        if axis == "x":
            return buf.at[c, x]
        if axis == "y":
            return buf.at[c, :, :, :, lax.rem(d // 2, 4)]
        return buf.at[c, :, d // 8, lax.rem(d, 2)]

    def moves(bufs, sems, orders, c, ph):
        axis = orders[c][ph]
        src, dst = bufs[ph], bufs[ph + 1]
        copies = [
            pltpu.make_async_copy(
                part(src, c, axis, me), part(dst, c, axis, me), sems[2].at[c, ph]
            )
        ]
        for n, peer in enumerate(peers[axis]):
            copies.append(
                pltpu.make_async_remote_copy(
                    src_ref=part(src, c, axis, peer),
                    dst_ref=part(dst, c, axis, me),
                    send_sem=sems[0].at[c, ph, n],
                    recv_sem=sems[1].at[c, ph, n],
                    device_id=peer,
                    device_id_type=MESH,
                )
            )
        return copies

    def begin(copies):
        for copy in copies:
            copy.start()

    def finish(copies):
        for copy in copies:
            copy.wait()

    there = ((fa, fb, fc, fd), (fs, fr, fl), ORDERS_THERE)
    back_way = ((ba, bb, bc, bd), (bs, br, bl), ORDERS_BACK)

    by_grid = sc.reshape(GRID + (16, T))

    def pack(buf, c):
        for k in range(2):
            for x in range(4):
                buf[c, x, :, k] = by_grid[:, :, k, x].astype(BF)

    def unpack(buf, c):
        for k in range(2):
            for x in range(4):
                by_grid[:, :, k, x] = buf[c, x, :, k].astype(F32)

    def prep(c):
        for a in range(3):
            load(c, a).wait()
        for r in range(LB):
            at = block_of(c, r)
            sc[:, r, :] = qv[:, at].astype(F32)
            sc[:, LB + r, :] = kv[:, at].astype(F32) * vv[:, at].astype(F32)
        pack(fa, c)

    def plan(c):
        load(c, 3).wait()
        unpack(fd, c)
        for r in range(LB):
            both = jnp.concatenate([sc[:, r, :], sc[:, LB + r, :]], axis=1).astype(BF)
            planned = dot(place[...], both)
            qp[c, :, lanes(r)] = planned[:, :T].astype(BF)
            up[c, :, lanes(r)] = planned[:, T:].astype(BF)
            grad = gv[:, block_of(c, r)].astype(F32)
            inn[c, :, lanes(r)] = (grad * planned[:, :T]).astype(BF)

    def halo(c):
        copies = []
        for n, (src, dst, to) in enumerate(((up, ear, 1), (inn, lat, 2))):
            copy = pltpu.make_async_remote_copy(
                src_ref=src.at[c],
                dst_ref=dst.at[c],
                send_sem=hs.at[c, n],
                recv_sem=hr.at[c, n],
                device_id=peers["x"][to],
                device_id_type=MESH,
            )
            copies.append(copy)
        return copies

    lane_group = iota(1, (1, T)) // 16

    def make(n, slot):
        rows = pl.ds(pl.multiple_of(n * 8, 8), 8)
        t = taps[rows]
        rt = rtaps[rows]
        for g in range(8):
            back = jnp.broadcast_to(rt[g : g + 1], (T, T))
            back = pltpu.roll(back, 0, 1, stride=1, stride_axis=0).astype(BF)
            ahead = jnp.broadcast_to(t[g : g + 1], (T, T))
            ahead = pltpu.roll(ahead, 0, 1, stride=1, stride_axis=0).astype(BF)
            w_sc[slot, lanes(g)] = jnp.concatenate([back, back], axis=1) * wmask[...]
            v_sc[slot, lanes(g)] = jnp.concatenate([ahead, ahead], axis=1) * vmask[...]

    def use(c, n, slot):
        at = pl.ds(pl.multiple_of(n * T, T), T)
        full = pl.ds(pl.multiple_of((c * LB + n) * T, T), T)
        u = up[c, :, at]
        inner_b = inn[c, :, at]
        u2 = jnp.concatenate([ear[c, :, at], u], axis=0)
        i2 = jnp.concatenate([inner_b, lat[c, :, at]], axis=0)
        f_all = dot(w_sc[slot], u2)
        d_all = dot(v_sc[slot], i2)
        turned = dot(flip, inner_b).astype(BF)
        zero = jnp.zeros((), BF)
        mine = jnp.concatenate([jnp.where(lane_group == g, turned, zero) for g in range(8)], axis=0)
        pairs = dot(mine, u2, ((1,), (1,)))
        f, d = f_all[:T], d_all[:T]
        lags = []
        for g in range(8):
            if g:
                f = jnp.where(lane_group == g, f_all[lanes(g)], f)
                d = jnp.where(lane_group == g, d_all[lanes(g)], d)
            p = pairs[lanes(g)]
            p = jnp.where(own_side, p[:, T:], p[:, :T]) * hmask[...]
            p = pltpu.roll(p, 1, 1, stride=1, stride_axis=0)
            lags.append(jnp.sum(p, axis=0, keepdims=True))
        gain = gain_ref[:, full]
        uf = u.astype(F32)
        qf = qp[c, :, at].astype(F32)
        gf = gv[:, full].astype(F32)
        inner = gf * qf
        gated = f + gain * uf
        gv[:, full] = (qf * gated).astype(BF)
        dq_sc[:, at] = (gf * gated).astype(BF)
        du_sc[:, at] = (d + gain * inner).astype(BF)
        skip = jnp.sum(inner * uf, axis=0, keepdims=True)
        other = pltpu.roll(skip, T // 2, 1)
        pad = jnp.zeros((3, T), F32)
        block = c * LB + n
        term[2 * block] = jnp.concatenate(lags[:4] + [skip, pad], axis=0)
        term[2 * block + 1] = jnp.concatenate(lags[4:] + [other, pad], axis=0)

    def conv(c):
        def step(j, carry):
            block = c * LB + 2 * j
            use(c, 2 * j, 0)
            make(block + 1, 1)
            use(c, 2 * j + 1, 1)
            make(lax.rem(block + 2, NCH * LB), 0)
            return carry

        lax.fori_loop(0, LB // 2, step, 0)
        for r in range(LB):
            both = jnp.concatenate([dq_sc[:, lanes(r)], du_sc[:, lanes(r)]], axis=1)
            back = dot(fetch[...], both)
            sc[:, r, :] = back[:, :T]
            sc[:, LB + r, :] = back[:, T:]
        pack(ba, c)

    def last(c):
        unpack(bd, c)
        for r in range(LB):
            at = block_of(c, r)
            qv[:, at] = sc[:, r, :].astype(BF)
            du = sc[:, LB + r, :]
            kf = kv[:, at].astype(F32)
            vf = vv[:, at].astype(F32)
            kv[:, at] = (du * vf).astype(BF)
            vv[:, at] = (du * kf).astype(BF)

    grid = term.reshape(GRID + (8, T))

    def term_moves(axis):
        view, slots, base = {
            "y": (lambda p: grid.at[:, lax.rem(p[0] // 2, 4)], ry, 0),
            "z": (lambda p: s1.at[p[0] // 8, lax.rem(p[0], 2)], rz, 3),
            "x": (lambda p: s2.at[p[1]], rx, 10),
        }[axis]
        return [
            pltpu.make_async_remote_copy(
                src_ref=view(peer), dst_ref=slots.at[n], send_sem=rs.at[base + n],
                recv_sem=rr.at[base + n], device_id=peer, device_id_type=MESH,
            )
            for n, peer in enumerate(peers[axis])
        ]

    def reduce(stage):
        if stage == 0:
            begin(term_moves("y"))
        elif stage == 1:
            finish(term_moves("y"))
            s1[...] = grid[:, y] + ry[0] + ry[1] + ry[2]
            begin(term_moves("z"))
        elif stage == 2:
            finish(term_moves("z"))
            total = s1[z, k]
            for n in range(7):
                total = total + rz[n]
            s2[...] = total
            begin(term_moves("x"))
        else:
            finish(term_moves("x"))
            total = s2[cx] + rx[0] + rx[1] + rx[2]
            hi = total.astype(BF)
            rest = total - hi.astype(F32)
            mid = rest.astype(BF)
            low = (rest - mid.astype(F32)).astype(BF)
            turned = dot(hi, mirror) + dot(mid, mirror) + dot(low, mirror)
            tokens = T * T
            filter_ref[...] = turned[:4] * (1 / math.sqrt(tokens * 16))
            skip_ref[...] = total[4:5, :64] * (1 / math.sqrt(tokens))

    def move(code):
        kind, c, ph = code // 100, code // 10 % 10, code % 10
        if kind == SET_UP and not c:
            load_rest()
            return
        if kind == SET_UP:
            set_up()
            make(0, 0)
            return
        if kind == MOVE_TERMS:
            reduce(ph)
            return
        way = there if kind == MOVE_THERE else back_way
        if ph:
            finish(moves(*way, c, ph - 1))
        if ph < 3:
            begin(moves(*way, c, ph))

    def work(kind, c):
        if kind == PREP:
            prep(c)
        elif kind == PLAN:
            plan(c)
            begin(halo(c))
        elif kind == CONV:
            finish(halo(c))
            conv(c)
        else:
            last(c)

    steps = [([], None)]
    for code in SCHEDULE:
        if code < 400:
            steps[-1] = (steps[-1][0], code // 100)
            steps.append(([], None))
        else:
            steps[-1][0].append(code)
    tail = steps.pop()[0]

    def choose(i, low, high):
        if not any(steps[n][0] for n in range(low, high)):
            return
        if high - low == 1:
            for code in steps[low][0]:
                move(code)
            return
        mid = (low + high) // 2
        pl.when(i < mid)(lambda: choose(i, low, mid))
        pl.when(i >= mid)(lambda: choose(i, mid, high))

    words = [
        sum(steps[n][1] << (2 * (n - first)) for n in range(first, min(first + 12, len(steps))))
        for first in range(0, len(steps), 12)
    ]

    def step(i, counts):
        choose(i, 0, len(steps))
        word = jnp.asarray(words[0], I32)
        for n in range(1, len(words)):
            word = jnp.where(i >= 12 * n, words[n], word)
        kind = lax.rem(lax.shift_right_logical(word, 2 * lax.rem(i, 12)), 4)
        for n in range(4):
            pl.when(kind == n)(lambda n=n: work(n, counts[n]))
        return tuple(counts[n] + (kind == n).astype(I32) for n in range(4))

    pl.semaphore_wait(barrier, sum(len(peers[axis]) for axis in "xyz"))
    zero_count = jnp.zeros((), I32)
    lax.fori_loop(0, len(steps), step, (zero_count,) * 4)
    for code in tail:
        move(code)


def hand_out(*refs):
    n = 6
    ins, outs, sems = refs[:n], refs[n : 2 * n], refs[-1]
    copies = []
    for a in range(4):
        for part in range(4):
            rows = pl.ds(part * 32, 32)
            copies.append(
                pltpu.make_async_copy(ins[a].at[rows], outs[a].at[rows], sems.at[a, part])
            )
    for copy in copies:
        copy.start()
    outs[4][...] = ins[4][...]
    outs[5][...] = ins[5][...]
    for copy in copies:
        copy.wait()


def body(q_rows, k_rows, v_rows, out_grad, filters, skip_gain, genome_len, plan_offset):
    chans = q_rows.shape[1]
    wide = (T, chans)
    act = pltpu.VMEM(wide, BF)
    anywhere = pl.BlockSpec(memory_space=pl.ANY)
    vmem = pl.BlockSpec(memory_space=pltpu.VMEM)
    smem = pl.BlockSpec(memory_space=pltpu.SMEM)
    flow = pltpu.VMEM((NCH, 4, 4, 2, 4, 16, T), BF)
    chunked = pltpu.VMEM((NCH, T, WIDE), BF)
    dma = pltpu.SemaphoreType.DMA
    groups = filters.shape[0]
    results = pl.pallas_call(
        mixer_kernel,
        in_specs=[anywhere] * 4 + [vmem, vmem, smem, vmem],
        out_specs=[vmem] * 6,
        out_shape=[act] * 4
        + [
            pltpu.VMEM((groups // T, T), F32),
            pltpu.VMEM((1, chans // T), F32),
        ],
        scratch_shapes=[flow] * 8
        + [chunked] * 5
        + [
            pltpu.VMEM((T, 2 * T), BF),
            pltpu.VMEM((T, 2 * T), BF),
            pltpu.VMEM((T, T), F32),
            pltpu.VMEM((T, T), BF),
            pltpu.VMEM((T, T), BF),
            pltpu.VMEM((groups, T), F32),
            pltpu.VMEM((groups, T), F32),
            pltpu.VMEM((2, 8 * T, 2 * T), BF),
            pltpu.VMEM((2, 8 * T, 2 * T), BF),
            pltpu.VMEM((T, 16, T), F32),
            pltpu.VMEM((T, WIDE), BF),
            pltpu.VMEM((T, WIDE), BF),
            pltpu.VMEM((T, 8, T), F32),
            pltpu.VMEM((3, 8, T), F32),
            pltpu.VMEM((3, 4, 2, 4, 8, T), F32),
            pltpu.VMEM((7, 4, 8, T), F32),
            pltpu.VMEM((4, 2, 4, 8, T), F32),
            pltpu.VMEM((4, 8, T), F32),
            dma((4, NCH)),
            dma((NCH, 3, 7)),
            dma((NCH, 3, 7)),
            dma((NCH, 3)),
            dma((NCH, 3, 7)),
            dma((NCH, 3, 7)),
            dma((NCH, 3)),
            dma((NCH, 2)),
            dma((NCH, 2)),
            dma((13,)),
            dma((13,)),
        ],
        compiler_params=pltpu.CompilerParams(
            collective_id=0, has_side_effects=True, vmem_limit_bytes=52 * 2**20
        ),
        name="mixer",
    )(
        q_rows, k_rows, v_rows, out_grad, filters, skip_gain.reshape(1, chans), genome_len,
        plan_offset.reshape(1, T),
    )
    *outs, skip_grad = pl.pallas_call(
        hand_out,
        in_specs=[vmem] * 6,
        out_specs=[anywhere] * 4 + [vmem] * 2,
        out_shape=[jax.ShapeDtypeStruct(r.shape, r.dtype) for r in results],
        scratch_shapes=[dma((4, 4))],
        compiler_params=pltpu.CompilerParams(vmem_limit_bytes=2 * 2**20),
        name="hand_out",
    )(*[pltpu.with_memory_space_constraint(r, pltpu.VMEM) for r in results])
    return (*outs, skip_grad.reshape(chans // T))


def solution(mesh):
    rows = P(("dp", "ctx"), None)
    return jax.shard_map(
        body,
        mesh=mesh,
        in_specs=(rows, rows, rows, rows, P(), P(), P("dp", None), P(None, ("dp", "ctx"), None)),
        out_specs=(rows, rows, rows, rows, rows, P(("dp", "ctx"))),
        check_vma=False,
    )
```
